256 devices in a mesh: rep: 4 (over x_hi, core), cplx: 4 (over y), row: 16 (over x_lo, z).
Axes of the slice: x: 4 (x_hi: 2, x_lo: 2; x = x_hi * 2 + x_lo), y: 4, z: 8, core: 2. Of those that a mesh axis runs over, the one named last changes fastest.
Arguments:
- pair_map: bfloat16 [16, 128, 128, 128], P(('rep', 'cplx'), 'row'), may hold values from -6 to 6
- cotangent: bfloat16 [16, 128, 128, 128], P(('rep', 'cplx'), 'row'), may hold values from -6 to 6
- residue_mask: int32 [16, 128], P(('rep', 'cplx')), may hold values from 0 to 1, as said below
- norm_outgo: float32 [128], replicated, may hold values from 0.25 to 1.75
- proj_outgo: bfloat16 [128, 640], replicated, may hold values from -0.5 to 0.5
- mid_outgo: float32 [128], replicated, may hold values from 0.25 to 1.75
- final_outgo: bfloat16 [128, 128], replicated, may hold values from -0.5 to 0.5
- norm_income: float32 [128], replicated, may hold values from 0.25 to 1.75
- proj_income: bfloat16 [128, 640], replicated, may hold values from -0.5 to 0.5
- mid_income: float32 [128], replicated, may hold values from 0.25 to 1.75
- final_income: bfloat16 [128, 128], replicated, may hold values from -0.5 to 0.5
Outputs:
- pair_grad: bfloat16 [16, 128, 128, 128], P(('rep', 'cplx'), 'row')
- norm_outgo_grad: float32 [128], replicated
- proj_outgo_grad: float32 [128, 640], replicated
- mid_outgo_grad: float32 [128], replicated
- final_outgo_grad: float32 [128, 128], replicated
- norm_income_grad: float32 [128], replicated
- proj_income_grad: float32 [128, 640], replicated
- mid_income_grad: float32 [128], replicated
- final_income_grad: float32 [128, 128], replicated
The draws below stay inside these ranges and needn't reach their ends.
Inputs may be any that keep to these rules, and one draw needn't show every extreme that they name: `residue_mask`: each complex's mask is 1 on a prefix of at least 64 residues and 0 after it.
All inputs are finite; a program needn't handle non-finite values.
Results may differ from the reference program's by a relative error of at most 0.025.
Values may be sent and summed in bfloat16 or wider, within the bound.
A program may use at most 128 MiB of HBM per device.

```python
import math
import jax
import jax.numpy as jnp
from jax import lax

C = 128
H = 128
N = 128
COMPLEXES = 16


def draw_residue_mask(key, part):
    key = jax.random.fold_in(key, 7)
    lengths = jax.random.randint(key, (COMPLEXES, 1), N // 2, N + 1)
    positions = jnp.arange(N, dtype=jnp.int32)[None, :]
    return (positions < lengths).astype(jnp.int32)


def steps_of(own_key, extent, split, least, largest):
    loudness = 1.0
    for position, blocks in split:
        heights = jax.random.uniform(jax.random.fold_in(jax.random.fold_in(own_key, 6), position), (blocks,), jnp.float32, least / len(split), largest / len(split))
        loudness = loudness * jnp.repeat(jnp.exp(heights), extent[position] // blocks).reshape((-1,) + (1,) * (len(extent) - 1 - position))
    return loudness


def noise(key, shape, scale, bound, cuts=(), held_as=jnp.bfloat16):
    factor_of = steps_of(key, shape, cuts, -0.22, 0.18) if cuts else 1.0
    values = jax.random.normal(key, shape, jnp.float32) * scale * factor_of
    return jnp.minimum(jnp.maximum(values, -bound), bound).astype(held_as)


def setup_inputs(seed: int = 0) -> dict:
    splits = jax.random.split(jax.random.key(seed), 12)
    pair_map = noise(splits[0], (COMPLEXES, N, N, C), 1.0, 6.0, ((0, 16), (1, 16)))
    cotangent = noise(splits[1], (COMPLEXES, N, N, C), 1.0, 6.0, ((0, 16), (1, 16)))
    residue_mask = draw_residue_mask(jax.random.fold_in(splits[11], 71), 0)
    norm_outgo = jnp.clip(1.0 + 0.15 * jax.random.normal(splits[3], (C,), jnp.float32), 0.25, 1.75)
    proj_outgo = noise(splits[4], (C, 4 * H + C), C ** -0.5, 0.5)
    mid_outgo = jnp.clip(1.0 + 0.15 * jax.random.normal(splits[5], (H,), jnp.float32), 0.25, 1.75)
    final_outgo = noise(splits[6], (H, C), H ** -0.5, 0.5)
    norm_income = jnp.clip(1.0 + 0.15 * jax.random.normal(splits[7], (C,), jnp.float32), 0.25, 1.75)
    proj_income = noise(splits[8], (C, 4 * H + C), C ** -0.5, 0.5)
    mid_income = jnp.clip(1.0 + 0.15 * jax.random.normal(splits[9], (H,), jnp.float32), 0.25, 1.75)
    final_income = noise(splits[10], (H, C), H ** -0.5, 0.5)
    return dict(pair_map=pair_map, cotangent=cotangent, residue_mask=residue_mask, norm_outgo=norm_outgo, proj_outgo=proj_outgo, mid_outgo=mid_outgo, final_outgo=final_outgo, norm_income=norm_income, proj_income=proj_income, mid_income=mid_income, final_income=final_income)


epsilon = 1e-05

def normalize(values):
    average = lax.optimization_barrier(jnp.mean(values, -1, keepdims=True))
    centered = values - average
    inv_std = lax.rsqrt(lax.optimization_barrier(jnp.mean(centered * centered, -1, keepdims=True)) + epsilon)
    return (centered * inv_std, inv_std)

def norm_back(grad_hat, standard, inv_std):
    first = lax.optimization_barrier(jnp.mean(grad_hat, -1, keepdims=True))
    second = lax.optimization_barrier(jnp.mean(grad_hat * standard, -1, keepdims=True))
    return inv_std * (grad_hat - first - standard * second)

def matmul(left, right):
    flat = left.reshape(-1, left.shape[-1])
    result = jnp.dot(flat, right, preferred_element_type=jnp.float32)
    return result.reshape(left.shape[:-1] + (right.shape[-1],))

def contract(left, right):
    flat_left = left.reshape(-1, left.shape[-1])
    flat_right = right.reshape(-1, right.shape[-1])
    return jnp.dot(flat_left.T, flat_right, preferred_element_type=jnp.float32)

def front_part(block, row_mask, col_mask, norm_gain, projection):
    width = norm_gain.shape[0]
    hidden = (projection.shape[1] - width) // 4
    standard, inv_std = normalize(block.astype(jnp.float32))
    normed = (standard * norm_gain).astype(jnp.bfloat16)
    projected = matmul(normed, projection)
    pair_mask = (row_mask[:, None] * col_mask[None, :])[..., None]
    left = (jax.nn.sigmoid(projected[..., :hidden]) * projected[..., hidden:2 * hidden] * pair_mask).astype(jnp.bfloat16)
    right = (jax.nn.sigmoid(projected[..., 2 * hidden:3 * hidden]) * projected[..., 3 * hidden:4 * hidden] * pair_mask).astype(jnp.bfloat16)
    gate_value = jax.nn.sigmoid(projected[..., 4 * hidden:])
    return (left, right, (normed, standard, inv_std, projected, gate_value, pair_mask))

def finish(product, mid_gain, final):
    prod_hat, mid_inv = normalize(product)
    middle = (prod_hat * mid_gain).astype(jnp.bfloat16)
    update = matmul(middle, final)
    return (update, (prod_hat, mid_inv, middle, update))

def upper_back(upstream, saved, kept, mid_gain, final):
    gate_value = saved[4]
    prod_hat, mid_inv, middle, update = kept
    incoming = upstream.astype(jnp.float32)
    grad_update = (gate_value * incoming).astype(jnp.bfloat16)
    grad_gate = incoming * update * gate_value * (1.0 - gate_value)
    grad_middle = matmul(grad_update, final.T)
    final_grad = contract(middle, grad_update)
    mid_grad = lax.optimization_barrier(jnp.sum((grad_middle * prod_hat).reshape(-1, prod_hat.shape[-1]), 0))
    grad_product = norm_back(grad_middle * mid_gain, prod_hat, mid_inv).astype(jnp.bfloat16)
    return (incoming, grad_gate, grad_product, final_grad, mid_grad)

def lower_back(incoming, grad_gate, grad_left, grad_right, saved, norm_gain, projection):
    normed, standard, inv_std, projected, gate_value, pair_mask = saved
    width = norm_gain.shape[0]
    hidden = (projection.shape[1] - width) // 4
    sig_left = jax.nn.sigmoid(projected[..., :hidden])
    sig_right = jax.nn.sigmoid(projected[..., 2 * hidden:3 * hidden])
    grad_proj = jnp.concatenate([grad_left * projected[..., hidden:2 * hidden] * pair_mask * sig_left * (1.0 - sig_left), grad_left * sig_left * pair_mask, grad_right * projected[..., 3 * hidden:4 * hidden] * pair_mask * sig_right * (1.0 - sig_right), grad_right * sig_right * pair_mask, grad_gate], -1).astype(jnp.bfloat16)
    proj_grad = contract(normed, grad_proj)
    grad_normed = matmul(grad_proj, projection.T)
    gain_grad = lax.optimization_barrier(jnp.sum((grad_normed * standard).reshape(-1, width), 0))
    block_grad = (incoming + norm_back(grad_normed * norm_gain, standard, inv_std)).astype(jnp.bfloat16)
    return (block_grad, gain_grad, proj_grad)

def triple(form, first, second):
    return jnp.einsum(form, first.astype(jnp.float32), second.astype(jnp.float32), precision=lax.Precision.HIGHEST)

def reference(pair_map, cotangent, residue_mask, norm_outgo, proj_outgo, mid_outgo, final_outgo, norm_income, proj_income, mid_income, final_income):

    def one_complex(items):
        block, upstream, mask_ints = items
        mask_float = mask_ints.astype(jnp.float32)
        left_one, right_one, saved_one = front_part(block, mask_float, mask_float, norm_outgo, proj_outgo)
        product_one = triple('ikc,jkc->ijc', left_one, right_one)
        update_one, kept_one = finish(product_one, mid_outgo, final_outgo)
        first_out = (block.astype(jnp.float32) + saved_one[4] * update_one).astype(jnp.bfloat16)
        left_two, right_two, saved_two = front_part(first_out, mask_float, mask_float, norm_income, proj_income)
        product_two = triple('kic,kjc->ijc', left_two, right_two)
        update_two, kept_two = finish(product_two, mid_income, final_income)
        incoming, grad_gate, grad_product, final_two, mid_two = upper_back(upstream, saved_two, kept_two, mid_income, final_income)
        grad_left = triple('ijc,kjc->kic', grad_product, right_two)
        grad_right = triple('kic,ijc->kjc', left_two, grad_product)
        first_grad, gain_two, proj_two = lower_back(incoming, grad_gate, grad_left, grad_right, saved_two, norm_income, proj_income)
        incoming, grad_gate, grad_product, final_one, mid_one = upper_back(first_grad, saved_one, kept_one, mid_outgo, final_outgo)
        grad_left = triple('ijc,jkc->ikc', grad_product, right_one)
        grad_right = triple('ijc,ikc->jkc', grad_product, left_one)
        block_grad, gain_one, proj_one = lower_back(incoming, grad_gate, grad_left, grad_right, saved_one, norm_outgo, proj_outgo)
        return (block_grad, (gain_one, proj_one, mid_one, final_one, gain_two, proj_two, mid_two, final_two))
    pair_grad, grads = lax.map(one_complex, (pair_map, cotangent, residue_mask))
    factor = 1.0 / math.sqrt(COMPLEXES * N * N)
    summed = [lax.optimization_barrier(jnp.sum(item, 0)) * factor for item in grads]
    return (pair_grad, summed[0], summed[1], summed[2], summed[3], summed[4], summed[5], summed[6], summed[7])
```

```python
import functools
import math

import jax
import jax.numpy as jnp
from jax import lax
from jax.experimental import pallas as pl
from jax.experimental.pallas import tpu as pltpu
from jax.sharding import PartitionSpec as P

EPS = 1e-05
MESH = pl.DeviceIdType.MESH
F32 = jnp.float32
BF16 = jnp.bfloat16
ROWS = 16
TILE = 128
OWN = 8


def nn(a, b):
    return lax.dot_general(a, b, (((1,), (0,)), ((), ())), preferred_element_type=F32)


def nt(a, b):
    return lax.dot_general(a, b, (((1,), (1,)), ((), ())), preferred_element_type=F32)


def turn(a):
    return a.astype(F32).T.astype(BF16)


def tn(a, b):
    return nn(turn(a), b)


def mean0(a):
    return jnp.mean(a, axis=0, keepdims=True)


def normalize(a):
    centered = a - mean0(a)
    inv = lax.rsqrt(mean0(centered * centered) + EPS)
    return centered * inv, inv


def norm_back(e, standard, inv):
    return inv * (e - mean0(e) - standard * mean0(e * standard))


def kernel(
    groups, cplx_size, factor,
    pm, ct, mask, n1, w1, m1, f1, n2, w2, m2, f2,
    out, o_n1, o_p1, o_m1, o_f1, o_n2, o_p2, o_m2, o_f2,
    wt, ft, ngain, mgain, col, rowm,
    xt, std, inv, nrm, cf, gate, ph, minv, mdl, upd, gup, gproj, inc,
    s_a, s_b, ch_l, ch_r,
    gacc, macc, pay, vec,
    send2, recv2, send1, recv1,
    a2s, a2r, b2s, b2r, c2s, c2r, a1s, a1r, b1s, b1r, c1s, c1r,
    ssem, rsem,
):
    me = lax.axis_index("row")
    my_x, my_z = me // 8, lax.rem(me, 8)
    my_rep, my_cplx = lax.axis_index("rep"), lax.axis_index("cplx")
    mq = my_rep * cplx_size + my_cplx

    def row_to(t):
        return lax.rem(my_x + t // 8, 2) * 8 + lax.rem(my_z + lax.rem(t, 8), 8)

    def row_from(t):
        return lax.rem(my_x + 2 - t // 8, 2) * 8 + lax.rem(my_z + 8 - lax.rem(t, 8), 8)

    def grp_to(t):
        return lax.rem(mq + t, groups)

    def grp_from(t):
        return lax.rem(mq + groups - t, groups)

    def row_id(d):
        return {"row": d}

    def grp_id(d):
        return {"rep": d // cplx_size, "cplx": lax.rem(d, cplx_size)}

    barrier = pltpu.get_barrier_semaphore()

    def greet_row(t, _):
        pl.semaphore_signal(barrier, inc=1, device_id=row_id(row_to(t)), device_id_type=MESH)
        return 0

    def greet_grp(t, _):
        pl.semaphore_signal(barrier, inc=1, device_id=grp_id(grp_to(t)), device_id_type=MESH)
        return 0

    lax.fori_loop(1, ROWS, greet_row, 0)
    lax.fori_loop(1, groups, greet_grp, 0)

    def row_copy(src, dst, phase, d, slot):
        return pltpu.make_async_remote_copy(
            src_ref=src, dst_ref=dst, send_sem=ssem.at[phase, d], recv_sem=rsem.at[phase, slot],
            device_id=row_id(d), device_id_type=MESH)

    def grp_copy(src, dst, phase, d, slot):
        return pltpu.make_async_remote_copy(
            src_ref=src, dst_ref=dst, send_sem=ssem.at[phase, d], recv_sem=rsem.at[phase, slot],
            device_id=grp_id(d), device_id_type=MESH)

    def lanes(i):
        return pl.ds(pl.multiple_of(i * TILE, TILE), TILE)

    def tiles(body):
        def step(i, _):
            body(i)
            return 0

        lax.fori_loop(0, OWN, step, 0)

    def scatter(stages, send, recv, phase):
        def rows_of(d):
            return pl.ds(pl.multiple_of(d * 64, 64), 64)

        for n, stage in enumerate(stages):
            recv[me, n * 64 : n * 64 + 64, :] = stage[rows_of(me), :].astype(BF16)

        def body(t, _):
            d = row_to(t)
            for n, stage in enumerate(stages):
                send[d, n * 64 : n * 64 + 64, :] = stage[rows_of(d), :].astype(BF16)
            row_copy(send.at[d], recv.at[me], phase, d, me).start()
            return 0

        lax.fori_loop(1, ROWS, body, 0)

    def give_back(send, recv, phase):
        recv[me] = send[me]

        def body(t, _):
            d = row_to(t)
            row_copy(send.at[d], recv.at[me], phase, d, me).start()
            return 0

        lax.fori_loop(1, ROWS, body, 0)

    def settle(send, recv, phase, each=None):
        if each is not None:
            each(me)

        def body(t, _):
            s = row_from(t)
            row_copy(send.at[s], recv.at[s], phase, s, s).wait()
            if each is not None:
                each(s)
            return 0

        lax.fori_loop(1, ROWS, body, 0)

    def unstage(recv, stages):
        def each(s):
            for n, stage in enumerate(stages):
                stage[pl.ds(pl.multiple_of(s * 64, 64), 64), :] = recv[
                    s, n * 64 : n * 64 + 64, :
                ].astype(F32)

        return each

    def strided(i):
        return pl.ds(i, TILE, stride=OWN)

    def pair_of(recv, base, p):
        block = recv[:, pl.ds(pl.multiple_of(base + 16 * p, 16), 16), :].astype(F32)
        return [block[:, 8 * n : 8 * n + 8, :].reshape(TILE, TILE).astype(BF16) for n in range(2)]

    def put_pair(send, base, p, pair):
        both = jnp.concatenate([m.reshape(ROWS, 8, TILE) for m in pair], axis=1)
        send[:, pl.ds(pl.multiple_of(base + 16 * p, 16), 16), :] = both.astype(BF16)

    def pairs(body):
        def step(p, _):
            body(p)
            return 0

        lax.fori_loop(0, 4, step, 0)

    def forward_channels(u, recv, send):
        def body(p):
            left, right = pair_of(recv, 0, p), pair_of(recv, 64, p)
            result = []
            for n in range(2):
                ch_l[u, 2 * p + n] = left[n]
                ch_r[u, 2 * p + n] = right[n]
                result.append(nt(left[n], right[n]) if u == 0 else tn(left[n], right[n]))
            put_pair(send, 0, p, result)

        pairs(body)

    def backward_channels(u, recv, send):
        def body(p):
            grads = pair_of(recv, 0, p)
            lefts, rights = [], []
            for n in range(2):
                left, right, grad = ch_l[u, 2 * p + n], ch_r[u, 2 * p + n], grads[n]
                if u == 0:
                    lefts.append(nn(grad, right))
                    rights.append(tn(grad, left))
                else:
                    lefts.append(nt(right, grad))
                    rights.append(nn(left, grad))
            put_pair(send, 0, p, lefts)
            put_pair(send, 64, p, rights)

        pairs(body)

    def front(u, i, x):
        standard, inv_std = normalize(x)
        std[u, i] = standard
        inv[u, i] = inv_std
        normed = (standard * ngain[u]).astype(BF16)
        nrm[u, :, lanes(i)] = normed
        projected = nn(wt[u], normed)
        pair_mask = rowm[i] * col[...]
        s = jax.nn.sigmoid(projected[0:128])
        left = s * projected[128:256] * pair_mask
        cf[u, 0, i] = left * (1.0 - s)
        cf[u, 1, i] = s * pair_mask
        s_a[strided(i), :] = left
        t = jax.nn.sigmoid(projected[256:384])
        right = t * projected[384:512] * pair_mask
        cf[u, 2, i] = right * (1.0 - t)
        cf[u, 3, i] = t * pair_mask
        s_b[strided(i), :] = right
        gate[u, i] = jax.nn.sigmoid(projected[512:640])

    def finish(u, i):
        prod_hat, mid_inv = normalize(s_a[strided(i), :])
        middle = (prod_hat * mgain[u]).astype(BF16)
        update = nn(ft[u], middle)
        ph[u, i] = prod_hat
        minv[u, i] = mid_inv
        mdl[u, :, lanes(i)] = middle
        upd[u, i] = update
        return update, prod_hat, mid_inv

    def upper(u, i, incoming, update, prod_hat, mid_inv, final):
        g = gate[u, i]
        inc[u, i] = incoming
        grad_update = (g * incoming).astype(BF16)
        gup[u, :, lanes(i)] = grad_update
        gproj[u, 512:640, lanes(i)] = (incoming * update * g * (1.0 - g)).astype(BF16)
        grad_middle = nn(final[...], grad_update)
        macc[u] += grad_middle * prod_hat
        s_b[strided(i), :] = norm_back(grad_middle * mgain[u], prod_hat, mid_inv)

    def lower(u, i, weight):
        grad_left, grad_right = s_a[strided(i), :], s_b[strided(i), :]
        gproj[u, 0:128, lanes(i)] = (grad_left * cf[u, 0, i]).astype(BF16)
        gproj[u, 128:256, lanes(i)] = (grad_left * cf[u, 1, i]).astype(BF16)
        gproj[u, 256:384, lanes(i)] = (grad_right * cf[u, 2, i]).astype(BF16)
        gproj[u, 384:512, lanes(i)] = (grad_right * cf[u, 3, i]).astype(BF16)
        grad_normed = nn(weight[...], gproj[u, :, lanes(i)])
        standard = std[u, i]
        gacc[u] += grad_normed * standard
        back = norm_back(grad_normed * ngain[u], standard, inv[u, i])
        return (inc[u, i] + back).astype(BF16)

    for u, (w, f, n, m) in enumerate(((w1, f1, n1, m1), (w2, f2, n2, m2))):
        for g in range(5):
            wt[u, g * 128 : g * 128 + 128, :] = turn(w[:, g * 128 : g * 128 + 128])
        ft[u] = turn(f[...])
        ngain[u] = jnp.broadcast_to(n[...], (TILE, TILE)).T
        mgain[u] = jnp.broadcast_to(m[...], (TILE, TILE)).T
        gacc[u] = jnp.zeros((TILE, TILE), F32)
        macc[u] = jnp.zeros((TILE, TILE), F32)
    col_mask = mask[...].astype(F32)
    col[...] = col_mask
    where = lax.broadcasted_iota(jnp.int32, (1, TILE), 1)
    for i in range(OWN):
        picked = jnp.sum(jnp.where(where == me * OWN + i, col_mask, 0.0), axis=1, keepdims=True)
        rowm[i] = jnp.broadcast_to(picked, (1, TILE))

    def first(i):
        x = pm[0, i].astype(F32).T
        xt[i] = x
        front(0, i, x)

    tiles(first)
    pl.semaphore_wait(barrier, ROWS - 1 + groups - 1)
    scatter((s_a, s_b), send2.at[0], recv2.at[0], 0)
    settle(send2.at[0], recv2.at[0], 0)
    forward_channels(0, recv2.at[0], send1.at[0])
    give_back(send1.at[0], recv1.at[0], 1)
    settle(send1.at[0], recv1.at[0], 1, unstage(recv1.at[0], (s_a,)))

    def second(i):
        update, _, _ = finish(0, i)
        first_out = (xt[i] + gate[0, i] * update).astype(BF16)
        front(1, i, first_out.astype(F32))

    tiles(second)
    scatter((s_a, s_b), send2.at[1], recv2.at[1], 2)
    settle(send2.at[1], recv2.at[1], 2)
    forward_channels(1, recv2.at[1], send1.at[1])
    give_back(send1.at[1], recv1.at[1], 3)
    settle(send1.at[1], recv1.at[1], 3, unstage(recv1.at[1], (s_a,)))

    def third(i):
        update, prod_hat, mid_inv = finish(1, i)
        upper(1, i, ct[0, i].astype(F32).T, update, prod_hat, mid_inv, f2)

    tiles(third)
    scatter((s_b,), send1.at[2], recv1.at[2], 4)
    pay[640:768, :] = nt(mdl[1], gup[1])
    settle(send1.at[2], recv1.at[2], 4)
    backward_channels(1, recv1.at[2], send2.at[2])
    give_back(send2.at[2], recv2.at[2], 5)
    settle(send2.at[2], recv2.at[2], 5, unstage(recv2.at[2], (s_a, s_b)))

    def fourth(i):
        first_grad = lower(1, i, w2).astype(F32)
        upper(0, i, first_grad, upd[0, i], ph[0, i], minv[0, i], f1)

    tiles(fourth)
    scatter((s_b,), send1.at[3], recv1.at[3], 6)

    def vectors(values):
        vec[...] = jnp.zeros(vec.shape, F32)
        for n, value in enumerate(values):
            vec[n : n + 1, :] = jnp.sum(value.T, axis=0, keepdims=True)

    def blocks_out(send, recv, phase, block):
        def fill(d, ref):
            ref[d, 0:block, :] = pay[pl.ds(pl.multiple_of(d * block, block), block), :].astype(BF16)
            ref[d, block : block + 16, :] = vec[...].astype(BF16)

        fill(mq, recv)

        def body(t, _):
            d = grp_to(t)
            fill(d, send)
            grp_copy(send.at[d], recv.at[mq], phase, d, mq).start()
            return 0

        lax.fori_loop(1, groups, body, 0)

    def blocks_in(send, recv, phase):
        def body(t, _):
            s = grp_from(t)
            grp_copy(send.at[s], recv.at[s], phase, s, s).wait()
            return 0

        lax.fori_loop(1, groups, body, 0)
        return jnp.sum(recv[...].astype(F32), axis=0)

    def whole_out(value, send, recv, phase):
        send[...] = value.astype(BF16)
        recv[me] = value.astype(BF16)

        def body(t, _):
            d = row_to(t)
            row_copy(send, recv.at[me], phase, d, me).start()
            return 0

        lax.fori_loop(1, ROWS, body, 0)

    def whole_in(send, recv, phase):
        def body(t, _):
            s = row_from(t)
            row_copy(send, recv.at[s], phase, s, s).wait()
            return 0

        lax.fori_loop(1, ROWS, body, 0)
        return jnp.sum(recv[...].astype(F32), axis=0)

    def back_out(value, send, recv, phase):
        send[...] = value.astype(BF16)
        recv[mq] = value.astype(BF16)

        def body(t, _):
            d = grp_to(t)
            grp_copy(send, recv.at[mq], phase, d, mq).start()
            return 0

        lax.fori_loop(1, groups, body, 0)

    def back_in(send, recv, phase):
        def body(t, _):
            s = grp_from(t)
            grp_copy(send, recv.at[s], phase, s, s).wait()
            return 0

        lax.fori_loop(1, groups, body, 0)

    proj = nt(nrm[1], gproj[1])
    for g in range(5):
        pay[g * 128 : g * 128 + 128, :] = proj[:, g * 128 : g * 128 + 128]
    pay[768:896, :] = nt(mdl[0], gup[0])
    pay[896:1024, :] = nt(nrm[0], gproj[0, 512:640, :])
    vectors((gacc[1], macc[1], macc[0]))
    blocks_out(a2s, a2r, 8, 64)

    settle(send1.at[3], recv1.at[3], 6)
    backward_channels(0, recv1.at[3], send2.at[3])
    give_back(send2.at[3], recv2.at[3], 7)
    whole_out(blocks_in(a2s, a2r, 8), b2s, b2r, 9)
    settle(send2.at[3], recv2.at[3], 7, unstage(recv2.at[3], (s_a, s_b)))

    def fifth(i):
        out[0, i] = lower(0, i, w1).astype(F32).T.astype(BF16)

    tiles(fifth)
    proj = nt(nrm[0], gproj[0, 0:512, :])
    for g in range(4):
        pay[g * 128 : g * 128 + 128, :] = proj[:, g * 128 : g * 128 + 128]
    vectors((gacc[0],))
    blocks_out(a1s, a1r, 11, 32)

    total = whole_in(b2s, b2r, 9)
    back_out(total[0:64], c2s, c2r, 10)
    o_n2[...] = total[64:65] * factor
    o_m2[...] = total[65:66] * factor
    o_m1[...] = total[66:67] * factor

    whole_out(blocks_in(a1s, a1r, 11), b1s, b1r, 12)
    back_in(c2s, c2r, 10)
    sums = c2r[...].reshape(1024, TILE).astype(F32) * factor
    for g in range(5):
        o_p2[:, g * 128 : g * 128 + 128] = sums[g * 128 : g * 128 + 128]
    o_f2[...] = sums[640:768]
    o_f1[...] = sums[768:896]
    o_p1[:, 512:640] = sums[896:1024]

    total = whole_in(b1s, b1r, 12)
    back_out(total[0:32], c1s, c1r, 13)
    o_n1[...] = total[32:33] * factor
    back_in(c1s, c1r, 13)
    sums = c1r[...].reshape(512, TILE).astype(F32) * factor
    for g in range(4):
        o_p1[:, g * 128 : g * 128 + 128] = sums[g * 128 : g * 128 + 128]


def on_device(groups, cplx_size, factor, pm, ct, mask, n1, w1, m1, f1, n2, w2, m2, f2):
    wide = (1, TILE)
    shapes = [
        (pm.shape, BF16),
        (wide, F32), ((TILE, 640), F32), (wide, F32), ((TILE, TILE), F32),
        (wide, F32), ((TILE, 640), F32), (wide, F32), ((TILE, TILE), F32),
    ]
    tile = (OWN, TILE, TILE)
    lane = (TILE, OWN * TILE)
    scratch = [
        pltpu.VMEM((2, 640, TILE), BF16),
        pltpu.VMEM((2, TILE, TILE), BF16),
        pltpu.VMEM((2, TILE, TILE), F32),
        pltpu.VMEM((2, TILE, TILE), F32),
        pltpu.VMEM(wide, F32),
        pltpu.VMEM((OWN, 1, TILE), F32),
        pltpu.VMEM(tile, F32),
        pltpu.VMEM((2,) + tile, F32),
        pltpu.VMEM((2, OWN, 1, TILE), F32),
        pltpu.VMEM((2,) + lane, BF16),
        pltpu.VMEM((2, 4) + tile, F32),
        pltpu.VMEM((2,) + tile, F32),
        pltpu.VMEM((2,) + tile, F32),
        pltpu.VMEM((2, OWN, 1, TILE), F32),
        pltpu.VMEM((2,) + lane, BF16),
        pltpu.VMEM((2,) + tile, F32),
        pltpu.VMEM((2,) + lane, BF16),
        pltpu.VMEM((2, 640, OWN * TILE), BF16),
        pltpu.VMEM((2,) + tile, F32),
        pltpu.VMEM((OWN * TILE, TILE), F32),
        pltpu.VMEM((OWN * TILE, TILE), F32),
        pltpu.VMEM((2,) + tile, BF16),
        pltpu.VMEM((2,) + tile, BF16),
        pltpu.VMEM((2, TILE, TILE), F32),
        pltpu.VMEM((2, TILE, TILE), F32),
        pltpu.VMEM((1024, TILE), F32),
        pltpu.VMEM((16, TILE), F32),
        pltpu.VMEM((4, ROWS, 128, TILE), BF16),
        pltpu.VMEM((4, ROWS, 128, TILE), BF16),
        pltpu.VMEM((4, ROWS, 64, TILE), BF16),
        pltpu.VMEM((4, ROWS, 64, TILE), BF16),
        pltpu.VMEM((16, 80, TILE), BF16),
        pltpu.VMEM((16, 80, TILE), BF16),
        pltpu.VMEM((80, TILE), BF16),
        pltpu.VMEM((ROWS, 80, TILE), BF16),
        pltpu.VMEM((64, TILE), BF16),
        pltpu.VMEM((16, 64, TILE), BF16),
        pltpu.VMEM((16, 48, TILE), BF16),
        pltpu.VMEM((16, 48, TILE), BF16),
        pltpu.VMEM((48, TILE), BF16),
        pltpu.VMEM((ROWS, 48, TILE), BF16),
        pltpu.VMEM((32, TILE), BF16),
        pltpu.VMEM((16, 32, TILE), BF16),
        pltpu.SemaphoreType.DMA((14, 16)),
        pltpu.SemaphoreType.DMA((14, 16)),
    ]
    vmem = pl.BlockSpec(memory_space=pltpu.VMEM)
    results = pl.pallas_call(
        functools.partial(kernel, groups, cplx_size, factor),
        out_shape=[jax.ShapeDtypeStruct(s, d) for s, d in shapes],
        in_specs=[vmem] * 11,
        out_specs=[vmem] * 9,
        scratch_shapes=scratch,
        compiler_params=pltpu.CompilerParams(
            collective_id=0, has_side_effects=True, vmem_limit_bytes=48 * 1024 * 1024
        ),
        name="triangle",
    )(
        pm, ct, mask,
        n1.reshape(wide), w1, m1.reshape(wide), f1,
        n2.reshape(wide), w2, m2.reshape(wide), f2,
    )
    flat = [r.reshape(TILE) if r.shape == wide else r for r in results]
    return tuple(flat)


def solution(mesh):
    groups = mesh.shape["rep"] * mesh.shape["cplx"]
    factor = 1.0 / math.sqrt(groups * TILE * TILE)
    blocks = P(("rep", "cplx"), "row", None, None)
    placed = (blocks, blocks, P(("rep", "cplx"), None)) + (P(),) * 8
    return jax.shard_map(
        functools.partial(on_device, groups, mesh.shape["cplx"], factor),
        mesh=mesh,
        in_specs=placed,
        out_specs=(blocks,) + (P(),) * 8,
        check_vma=False,
    )
```

```python
import functools
import math

import jax
import jax.numpy as jnp
from jax import lax
from jax.experimental import pallas as pl
from jax.experimental.pallas import tpu as pltpu
from jax.sharding import PartitionSpec as P

EPS = 1e-05
MESH = pl.DeviceIdType.MESH
F32 = jnp.float32
BF16 = jnp.bfloat16
ROWS = 16
TILE = 128
VMEM_BYTES = 63 * 1024 * 1024
OWN = 8


def nn(a, b):
    return lax.dot_general(a, b, (((1,), (0,)), ((), ())), preferred_element_type=F32)


def nt(a, b):
    return lax.dot_general(a, b, (((1,), (1,)), ((), ())), preferred_element_type=F32)


def turn(a):
    return a.astype(F32).T.astype(BF16)


def tn(a, b):
    return nn(turn(a), b)


def mean0(a):
    return jnp.mean(a, axis=0, keepdims=True)


def normalize(a):
    centered = a - mean0(a)
    inv = lax.rsqrt(mean0(centered * centered) + EPS)
    return centered * inv, inv


def norm_back(e, standard, inv):
    return inv * (e - mean0(e) - standard * mean0(e * standard))


def kernel(
    groups, cplx_size, factor,
    pm_in, ct_in, mask_in, n1_in, w1_in, m1_in, f1_in, n2_in, w2_in, m2_in, f2_in,
    out_to, n1_to, p1_to, m1_to, f1_to, n2_to, p2_to, m2_to, f2_to,
    pm, ct, mask, n1, w1, m1, f1, n2, w2, m2, f2,
    out, o_n1, o_p1, o_m1, o_f1, o_n2, o_p2, o_m2, o_f2,
    wt, ft, ngain, mgain, col, rowm,
    xt, std, inv, nrm, cf, gate, ph, minv, mdl, upd, gup, gproj, inc,
    s_a, s_b, ch_l, ch_r,
    gacc, macc, pay, vec,
    send2, recv2, send1, recv1,
    a2s, a2r, b2s, b2r, c2s, c2r, a1s, a1r, b1s, b1r, c1s, c1r,
    ssem, rsem, isem, osem,
):
    me = lax.axis_index("row")
    my_x, my_z = me // 8, lax.rem(me, 8)
    my_rep, my_cplx = lax.axis_index("rep"), lax.axis_index("cplx")
    mq = my_rep * cplx_size + my_cplx

    def offsets(t):
        n = lax.rem(t - 1, 8)
        return 1 - (t - 1) // 8, lax.rem(12 + (2 * lax.rem(n, 2) - 1) * ((n + 1) // 2), 8)

    def row_to(t):
        dx, dz = offsets(t)
        return lax.rem(my_x + dx, 2) * 8 + lax.rem(my_z + dz, 8)

    def row_from(t):
        dx, dz = offsets(t)
        return lax.rem(my_x + dx, 2) * 8 + lax.rem(my_z + 8 - dz, 8)

    def grp_to(t):
        return lax.rem(mq + t, groups)

    def grp_from(t):
        return lax.rem(mq + groups - t, groups)

    def row_id(d):
        return {"row": d}

    def grp_id(d):
        return {"rep": d // cplx_size, "cplx": lax.rem(d, cplx_size)}

    barrier = pltpu.get_barrier_semaphore()

    def greet_row(t, _):
        pl.semaphore_signal(barrier, inc=1, device_id=row_id(row_to(t)), device_id_type=MESH)
        return 0

    def greet_grp(t, _):
        pl.semaphore_signal(barrier, inc=1, device_id=grp_id(grp_to(t)), device_id_type=MESH)
        return 0

    loads = [
        pltpu.make_async_copy(a, b, isem.at[n])
        for n, (a, b) in enumerate((
            (pm_in, pm), (w1_in, w1), (n1_in, n1), (mask_in, mask),
            (f1_in, f1), (m1_in, m1), (w2_in, w2), (n2_in, n2),
            (f2_in, f2), (m2_in, m2), (ct_in, ct),
        ))
    ]
    for load in loads:
        load.start()
    lax.fori_loop(1, ROWS, greet_row, 0)
    lax.fori_loop(1, groups, greet_grp, 0)

    def row_copy(src, dst, phase, d, slot):
        return pltpu.make_async_remote_copy(
            src_ref=src, dst_ref=dst, send_sem=ssem.at[phase, d], recv_sem=rsem.at[phase, slot],
            device_id=row_id(d), device_id_type=MESH)

    def grp_copy(src, dst, phase, d, slot):
        return pltpu.make_async_remote_copy(
            src_ref=src, dst_ref=dst, send_sem=ssem.at[phase, d], recv_sem=rsem.at[phase, slot],
            device_id=grp_id(d), device_id_type=MESH)

    def lanes(i):
        return pl.ds(pl.multiple_of(i * TILE, TILE), TILE)

    def tiles(body):
        def step(i, _):
            body(i)
            return 0

        lax.fori_loop(0, OWN, step, 0, unroll=4)

    def scatter(stages, send, recv, phase):
        def rows_of(d):
            return pl.ds(pl.multiple_of(d * 64, 64), 64)

        for n, stage in enumerate(stages):
            recv[me, n * 64 : n * 64 + 64, :] = stage[rows_of(me), :].astype(BF16)

        def body(t, _):
            d = row_to(t)
            for n, stage in enumerate(stages):
                send[d, n * 64 : n * 64 + 64, :] = stage[rows_of(d), :].astype(BF16)
            row_copy(send.at[d], recv.at[me], phase, d, me).start()
            return 0

        lax.fori_loop(1, ROWS, body, 0)

    def give_back(send, recv, phase):
        recv[me] = send[me]

        def body(t, _):
            d = row_to(t)
            row_copy(send.at[d], recv.at[me], phase, d, me).start()
            return 0

        lax.fori_loop(1, ROWS, body, 0)

    def settle(send, recv, phase, each=None):
        if each is not None:
            each(me)

        def body(t, _):
            s = row_from(t)
            row_copy(send.at[s], recv.at[s], phase, s, s).wait()
            if each is not None:
                each(s)
            return 0

        lax.fori_loop(1, ROWS, body, 0)

    def unstage(recv, stages):
        def each(s):
            for n, stage in enumerate(stages):
                stage[pl.ds(pl.multiple_of(s * 64, 64), 64), :] = recv[
                    s, n * 64 : n * 64 + 64, :
                ].astype(F32)

        return each

    def strided(i):
        return pl.ds(i, TILE, stride=OWN)

    def pair_of(recv, base, p):
        block = recv[:, pl.ds(pl.multiple_of(base + 16 * p, 16), 16), :].astype(F32)
        return [block[:, 8 * n : 8 * n + 8, :].reshape(TILE, TILE).astype(BF16) for n in range(2)]

    def put_pair(send, base, p, pair):
        both = jnp.concatenate([m.reshape(ROWS, 8, TILE) for m in pair], axis=1)
        send[:, pl.ds(pl.multiple_of(base + 16 * p, 16), 16), :] = both.astype(BF16)

    def pairs(body):
        def step(p, _):
            body(p)
            return 0

        lax.fori_loop(0, 4, step, 0, unroll=2)

    def forward_channels(u, recv, send):
        def body(p):
            left, right = pair_of(recv, 0, p), pair_of(recv, 64, p)
            result = []
            for n in range(2):
                ch_l[u, 2 * p + n] = left[n]
                ch_r[u, 2 * p + n] = right[n]
                result.append(nt(left[n], right[n]) if u == 0 else tn(left[n], right[n]))
            put_pair(send, 0, p, result)

        pairs(body)

    def backward_channels(u, recv, send):
        def body(p):
            grads = pair_of(recv, 0, p)
            lefts, rights = [], []
            for n in range(2):
                left, right, grad = ch_l[u, 2 * p + n], ch_r[u, 2 * p + n], grads[n]
                if u == 0:
                    lefts.append(nn(grad, right))
                    rights.append(tn(grad, left))
                else:
                    lefts.append(nt(right, grad))
                    rights.append(nn(left, grad))
            put_pair(send, 0, p, lefts)
            put_pair(send, 64, p, rights)

        pairs(body)

    def front(u, i, x):
        standard, inv_std = normalize(x)
        std[u, i] = standard
        inv[u, i] = inv_std
        normed = (standard * ngain[u]).astype(BF16)
        nrm[u, :, lanes(i)] = normed
        projected = nn(wt[u], normed)
        pair_mask = rowm[i] * col[...]
        s = jax.nn.sigmoid(projected[0:128])
        left = s * projected[128:256] * pair_mask
        cf[u, 0, i] = left * (1.0 - s)
        cf[u, 1, i] = s * pair_mask
        s_a[strided(i), :] = left
        t = jax.nn.sigmoid(projected[256:384])
        right = t * projected[384:512] * pair_mask
        cf[u, 2, i] = right * (1.0 - t)
        cf[u, 3, i] = t * pair_mask
        s_b[strided(i), :] = right
        gate[u, i] = jax.nn.sigmoid(projected[512:640])

    def finish(u, i):
        prod_hat, mid_inv = normalize(s_a[strided(i), :])
        middle = (prod_hat * mgain[u]).astype(BF16)
        update = nn(ft[u], middle)
        ph[u, i] = prod_hat
        minv[u, i] = mid_inv
        mdl[u, :, lanes(i)] = middle
        upd[u, i] = update
        return update, prod_hat, mid_inv

    def upper(u, i, incoming, update, prod_hat, mid_inv, final):
        g = gate[u, i]
        inc[u, i] = incoming
        grad_update = (g * incoming).astype(BF16)
        gup[u, :, lanes(i)] = grad_update
        gproj[u, 512:640, lanes(i)] = (incoming * update * g * (1.0 - g)).astype(BF16)
        grad_middle = nn(final[...], grad_update)
        macc[u] += grad_middle * prod_hat
        s_b[strided(i), :] = norm_back(grad_middle * mgain[u], prod_hat, mid_inv)

    def lower(u, i, weight):
        grad_left, grad_right = s_a[strided(i), :], s_b[strided(i), :]
        gproj[u, 0:128, lanes(i)] = (grad_left * cf[u, 0, i]).astype(BF16)
        gproj[u, 128:256, lanes(i)] = (grad_left * cf[u, 1, i]).astype(BF16)
        gproj[u, 256:384, lanes(i)] = (grad_right * cf[u, 2, i]).astype(BF16)
        gproj[u, 384:512, lanes(i)] = (grad_right * cf[u, 3, i]).astype(BF16)
        grad_normed = nn(weight[...], gproj[u, :, lanes(i)])
        standard = std[u, i]
        gacc[u] += grad_normed * standard
        back = norm_back(grad_normed * ngain[u], standard, inv[u, i])
        return (inc[u, i] + back).astype(BF16)

    def spread(row):
        return jnp.broadcast_to(row[...], (TILE, TILE)).T

    def weights(u, w, n):
        for g in range(5):
            wt[u, g * 128 : g * 128 + 128, :] = turn(w[:, g * 128 : g * 128 + 128])
        ngain[u] = spread(n)

    for load in loads[0:4]:
        load.wait()
    weights(0, w1, n1)
    col_mask = mask[...].astype(F32)
    col[...] = col_mask
    where = lax.broadcasted_iota(jnp.int32, (1, TILE), 1)
    for i in range(OWN):
        picked = jnp.sum(jnp.where(where == me * OWN + i, col_mask, 0.0), axis=1, keepdims=True)
        rowm[i] = jnp.broadcast_to(picked, (1, TILE))

    def first(i):
        x = pm[0, i].astype(F32).T
        xt[i] = x
        front(0, i, x)

    tiles(first)
    pl.semaphore_wait(barrier, ROWS - 1 + groups - 1)
    scatter((s_a, s_b), send2.at[0], recv2.at[0], 0)
    for load in loads[4:]:
        load.wait()
    weights(1, w2, n2)
    for u, (f, m) in enumerate(((f1, m1), (f2, m2))):
        ft[u] = turn(f[...])
        mgain[u] = spread(m)
        gacc[u] = jnp.zeros((TILE, TILE), F32)
        macc[u] = jnp.zeros((TILE, TILE), F32)
    settle(send2.at[0], recv2.at[0], 0)
    forward_channels(0, recv2.at[0], send1.at[0])
    give_back(send1.at[0], recv1.at[0], 1)
    settle(send1.at[0], recv1.at[0], 1, unstage(recv1.at[0], (s_a,)))

    def second(i):
        update, _, _ = finish(0, i)
        first_out = (xt[i] + gate[0, i] * update).astype(BF16)
        front(1, i, first_out.astype(F32))

    tiles(second)
    scatter((s_a, s_b), send2.at[1], recv2.at[1], 2)
    settle(send2.at[1], recv2.at[1], 2)
    forward_channels(1, recv2.at[1], send1.at[1])
    give_back(send1.at[1], recv1.at[1], 3)
    settle(send1.at[1], recv1.at[1], 3, unstage(recv1.at[1], (s_a,)))

    def third(i):
        update, prod_hat, mid_inv = finish(1, i)
        upper(1, i, ct[0, i].astype(F32).T, update, prod_hat, mid_inv, f2)

    tiles(third)
    scatter((s_b,), send1.at[2], recv1.at[2], 4)
    pay[640:768, :] = nt(mdl[1], gup[1])
    settle(send1.at[2], recv1.at[2], 4)
    backward_channels(1, recv1.at[2], send2.at[2])
    give_back(send2.at[2], recv2.at[2], 5)
    settle(send2.at[2], recv2.at[2], 5, unstage(recv2.at[2], (s_a, s_b)))

    def fourth(i):
        first_grad = lower(1, i, w2).astype(F32)
        upper(0, i, first_grad, upd[0, i], ph[0, i], minv[0, i], f1)

    tiles(fourth)
    scatter((s_b,), send1.at[3], recv1.at[3], 6)

    def vectors(values):
        vec[...] = jnp.zeros(vec.shape, F32)
        for n, value in enumerate(values):
            vec[n : n + 1, :] = jnp.sum(value.T, axis=0, keepdims=True)

    def blocks_out(send, recv, phase, block):
        def fill(d, ref):
            ref[d, 0:block, :] = pay[pl.ds(pl.multiple_of(d * block, block), block), :].astype(BF16)
            ref[d, block : block + 16, :] = vec[...].astype(BF16)

        fill(mq, recv)

        def body(t, _):
            d = grp_to(t)
            fill(d, send)
            grp_copy(send.at[d], recv.at[mq], phase, d, mq).start()
            return 0

        lax.fori_loop(1, groups, body, 0)

    def blocks_in(send, recv, phase):
        def body(t, _):
            s = grp_from(t)
            grp_copy(send.at[s], recv.at[s], phase, s, s).wait()
            return 0

        lax.fori_loop(1, groups, body, 0)
        return jnp.sum(recv[...].astype(F32), axis=0)

    def whole_out(value, send, recv, phase):
        send[...] = value.astype(BF16)
        recv[me] = value.astype(BF16)

        def body(t, _):
            d = row_to(t)
            row_copy(send, recv.at[me], phase, d, me).start()
            return 0

        lax.fori_loop(1, ROWS, body, 0)

    def whole_in(send, recv, phase):
        def body(t, _):
            s = row_from(t)
            row_copy(send, recv.at[s], phase, s, s).wait()
            return 0

        lax.fori_loop(1, ROWS, body, 0)
        return jnp.sum(recv[...].astype(F32), axis=0)

    def back_out(value, send, recv, phase):
        send[...] = value.astype(BF16)
        recv[mq] = value.astype(BF16)

        def body(t, _):
            d = grp_to(t)
            grp_copy(send, recv.at[mq], phase, d, mq).start()
            return 0

        lax.fori_loop(1, groups, body, 0)

    def back_in(send, recv, phase):
        def body(t, _):
            s = grp_from(t)
            grp_copy(send, recv.at[s], phase, s, s).wait()
            return 0

        lax.fori_loop(1, groups, body, 0)

    proj = nt(nrm[1], gproj[1])
    for g in range(5):
        pay[g * 128 : g * 128 + 128, :] = proj[:, g * 128 : g * 128 + 128]
    pay[768:896, :] = nt(mdl[0], gup[0])
    pay[896:1024, :] = nt(nrm[0], gproj[0, 512:640, :])
    vectors((gacc[1], macc[1], macc[0]))
    blocks_out(a2s, a2r, 8, 64)

    settle(send1.at[3], recv1.at[3], 6)
    backward_channels(0, recv1.at[3], send2.at[3])
    give_back(send2.at[3], recv2.at[3], 7)
    whole_out(blocks_in(a2s, a2r, 8), b2s, b2r, 9)
    settle(send2.at[3], recv2.at[3], 7, unstage(recv2.at[3], (s_a, s_b)))

    def fifth(i):
        out[0, i] = lower(0, i, w1).astype(F32).T.astype(BF16)

    tiles(fifth)
    stores = [pltpu.make_async_copy(out, out_to, osem.at[0])]
    stores[0].start()

    def store(n, a, b):
        stores.append(pltpu.make_async_copy(a, b, osem.at[n]))
        stores[-1].start()

    proj = nt(nrm[0], gproj[0, 0:512, :])
    for g in range(4):
        pay[g * 128 : g * 128 + 128, :] = proj[:, g * 128 : g * 128 + 128]
    vectors((gacc[0],))
    blocks_out(a1s, a1r, 11, 32)

    total = whole_in(b2s, b2r, 9)
    back_out(total[0:64], c2s, c2r, 10)
    o_n2[...] = total[64:65] * factor
    o_m2[...] = total[65:66] * factor
    o_m1[...] = total[66:67] * factor
    store(1, o_n2, n2_to)
    store(2, o_m2, m2_to)
    store(3, o_m1, m1_to)

    whole_out(blocks_in(a1s, a1r, 11), b1s, b1r, 12)
    back_in(c2s, c2r, 10)
    sums = c2r[...].reshape(1024, TILE).astype(F32) * factor
    for g in range(5):
        o_p2[:, g * 128 : g * 128 + 128] = sums[g * 128 : g * 128 + 128]
    o_f2[...] = sums[640:768]
    o_f1[...] = sums[768:896]
    o_p1[:, 512:640] = sums[896:1024]
    store(4, o_p2, p2_to)
    store(5, o_f2, f2_to)
    store(6, o_f1, f1_to)

    total = whole_in(b1s, b1r, 12)
    back_out(total[0:32], c1s, c1r, 13)
    o_n1[...] = total[32:33] * factor
    store(7, o_n1, n1_to)
    back_in(c1s, c1r, 13)
    sums = c1r[...].reshape(512, TILE).astype(F32) * factor
    for g in range(4):
        o_p1[:, g * 128 : g * 128 + 128] = sums[g * 128 : g * 128 + 128]

    store(8, o_p1, p1_to)
    for copy in stores:
        copy.wait()


def hand_on(*refs):
    froms, tos, held, sems = refs[:9], refs[9:18], refs[18:27], refs[27]
    loads = [pltpu.make_async_copy(a, b, sems.at[0, n]) for n, (a, b) in enumerate(zip(froms, held))]
    stores = [pltpu.make_async_copy(a, b, sems.at[1, n]) for n, (a, b) in enumerate(zip(held, tos))]
    for load in loads:
        load.start()
    for load, store in zip(loads, stores):
        load.wait()
        store.start()
    for store in stores:
        store.wait()


def on_device(groups, cplx_size, factor, pm, ct, mask, n1, w1, m1, f1, n2, w2, m2, f2):
    wide = (1, TILE)
    shapes = [
        (pm.shape, BF16),
        (wide, F32), ((TILE, 640), F32), (wide, F32), ((TILE, TILE), F32),
        (wide, F32), ((TILE, 640), F32), (wide, F32), ((TILE, TILE), F32),
    ]
    tile = (OWN, TILE, TILE)
    lane = (TILE, OWN * TILE)
    loaded = [
        (pm.shape, BF16), (ct.shape, BF16), (mask.shape, jnp.int32),
        (wide, F32), ((TILE, 640), BF16), (wide, F32), ((TILE, TILE), BF16),
        (wide, F32), ((TILE, 640), BF16), (wide, F32), ((TILE, TILE), BF16),
    ]
    scratch = [pltpu.VMEM(s, d) for s, d in loaded + shapes] + [
        pltpu.VMEM((2, 640, TILE), BF16),
        pltpu.VMEM((2, TILE, TILE), BF16),
        pltpu.VMEM((2, TILE, TILE), F32),
        pltpu.VMEM((2, TILE, TILE), F32),
        pltpu.VMEM(wide, F32),
        pltpu.VMEM((OWN, 1, TILE), F32),
        pltpu.VMEM(tile, F32),
        pltpu.VMEM((2,) + tile, F32),
        pltpu.VMEM((2, OWN, 1, TILE), F32),
        pltpu.VMEM((2,) + lane, BF16),
        pltpu.VMEM((2, 4) + tile, F32),
        pltpu.VMEM((2,) + tile, F32),
        pltpu.VMEM((2,) + tile, F32),
        pltpu.VMEM((2, OWN, 1, TILE), F32),
        pltpu.VMEM((2,) + lane, BF16),
        pltpu.VMEM((2,) + tile, F32),
        pltpu.VMEM((2,) + lane, BF16),
        pltpu.VMEM((2, 640, OWN * TILE), BF16),
        pltpu.VMEM((2,) + tile, F32),
        pltpu.VMEM((OWN * TILE, TILE), F32),
        pltpu.VMEM((OWN * TILE, TILE), F32),
        pltpu.VMEM((2,) + tile, BF16),
        pltpu.VMEM((2,) + tile, BF16),
        pltpu.VMEM((2, TILE, TILE), F32),
        pltpu.VMEM((2, TILE, TILE), F32),
        pltpu.VMEM((1024, TILE), F32),
        pltpu.VMEM((16, TILE), F32),
        pltpu.VMEM((4, ROWS, 128, TILE), BF16),
        pltpu.VMEM((4, ROWS, 128, TILE), BF16),
        pltpu.VMEM((4, ROWS, 64, TILE), BF16),
        pltpu.VMEM((4, ROWS, 64, TILE), BF16),
        pltpu.VMEM((16, 80, TILE), BF16),
        pltpu.VMEM((16, 80, TILE), BF16),
        pltpu.VMEM((80, TILE), BF16),
        pltpu.VMEM((ROWS, 80, TILE), BF16),
        pltpu.VMEM((64, TILE), BF16),
        pltpu.VMEM((16, 64, TILE), BF16),
        pltpu.VMEM((16, 48, TILE), BF16),
        pltpu.VMEM((16, 48, TILE), BF16),
        pltpu.VMEM((48, TILE), BF16),
        pltpu.VMEM((ROWS, 48, TILE), BF16),
        pltpu.VMEM((32, TILE), BF16),
        pltpu.VMEM((16, 32, TILE), BF16),
        pltpu.SemaphoreType.DMA((14, 16)),
        pltpu.SemaphoreType.DMA((14, 16)),
        pltpu.SemaphoreType.DMA((11,)),
        pltpu.SemaphoreType.DMA((9,)),
    ]
    anywhere = pl.BlockSpec(memory_space=pl.ANY)
    results = pl.pallas_call(
        functools.partial(kernel, groups, cplx_size, factor),
        out_shape=[jax.ShapeDtypeStruct(s, d) for s, d in shapes],
        in_specs=[anywhere] * 11,
        out_specs=[anywhere] * 9,
        scratch_shapes=scratch,
        compiler_params=pltpu.CompilerParams(
            collective_id=0, has_side_effects=True, vmem_limit_bytes=VMEM_BYTES
        ),
        name="triangle",
    )(
        pm, ct, mask,
        n1.reshape(wide), w1, m1.reshape(wide), f1,
        n2.reshape(wide), w2, m2.reshape(wide), f2,
    )
    results = pl.pallas_call(
        hand_on,
        out_shape=[jax.ShapeDtypeStruct(s, d) for s, d in shapes],
        in_specs=[anywhere] * 9,
        out_specs=[anywhere] * 9,
        scratch_shapes=[pltpu.VMEM(s, d) for s, d in shapes] + [pltpu.SemaphoreType.DMA((2, 9))],
        compiler_params=pltpu.CompilerParams(vmem_limit_bytes=VMEM_BYTES),
        name="hand_on",
    )(*results)
    flat = [r.reshape(TILE) if r.shape == wide else r for r in results]
    return tuple(flat)


def solution(mesh):
    groups = mesh.shape["rep"] * mesh.shape["cplx"]
    factor = 1.0 / math.sqrt(groups * TILE * TILE)
    blocks = P(("rep", "cplx"), "row", None, None)
    placed = (blocks, blocks, P(("rep", "cplx"), None)) + (P(),) * 8
    return jax.shard_map(
        functools.partial(on_device, groups, mesh.shape["cplx"], factor),
        mesh=mesh,
        in_specs=placed,
        out_specs=(blocks,) + (P(),) * 8,
        check_vma=False,
    )
```

```python
import functools
import math

import jax
import jax.numpy as jnp
from jax import lax
from jax.experimental import pallas as pl
from jax.experimental.pallas import tpu as pltpu
from jax.sharding import PartitionSpec as P

EPS = 1e-05
MESH = pl.DeviceIdType.MESH
F32 = jnp.float32
BF16 = jnp.bfloat16
ROWS = 16
TILE = 128
VMEM_BYTES = 63 * 1024 * 1024
OWN = 8
PART = 4


def nn(a, b):
    return lax.dot_general(a, b, (((1,), (0,)), ((), ())), preferred_element_type=F32)


def nt(a, b):
    return lax.dot_general(a, b, (((1,), (1,)), ((), ())), preferred_element_type=F32)


def turn(a):
    return a.astype(F32).T.astype(BF16)


def tn(a, b):
    return nn(turn(a), b)


def mean0(a):
    return jnp.mean(a, axis=0, keepdims=True)


def normalize(a):
    centered = a - mean0(a)
    inv = lax.rsqrt(mean0(centered * centered) + EPS)
    return centered * inv, inv


def norm_back(e, standard, inv):
    return inv * (e - mean0(e) - standard * mean0(e * standard))


def kernel(
    groups, factor,
    pm_in, ct_in, mask_in, n1_in, w1_in, m1_in, f1_in, n2_in, w2_in, m2_in, f2_in,
    out_to, n1_to, p1_to, m1_to, f1_to, n2_to, p2_to, m2_to, f2_to,
    pm, ct, masks, n1, w1, m1, f1, n2, w2, m2, f2,
    out, o_n1, o_p1, o_m1, o_f1, o_n2, o_p2, o_m2, o_f2,
    wt, ft, ngain, mgain, rowm,
    xt, std, inv, nrm, cf, gate, ph, minv, mdl, upd, gup, gproj, inc,
    s_a, s_b, ch_l, ch_r,
    gacc, macc, pay, vec,
    send2, recv2, send1, recv1,
    a2s, a2r, b2s, b2r, c2s, c2r, a1s, a1r, b1s, b1r, c1s, c1r,
    ssem, rsem, isem, osem, xsem, ysem,
):
    me = lax.axis_index("row")
    my_x, my_z = me // 8, lax.rem(me, 8)
    my_rep, my_cplx = lax.axis_index("rep"), lax.axis_index("cplx")
    side, core = my_rep // 2, lax.rem(my_rep, 2)
    mate = 1 - core
    mq = my_rep * 4 + my_cplx

    def offsets(t):
        n = lax.rem(t - 1, 8)
        return 1 - (t - 1) // 8, lax.rem(12 + (2 * lax.rem(n, 2) - 1) * ((n + 1) // 2), 8)

    def row_to(t):
        dx, dz = offsets(t)
        return lax.rem(my_x + dx, 2) * 8 + lax.rem(my_z + dz, 8)

    def row_from(t):
        dx, dz = offsets(t)
        return lax.rem(my_x + dx, 2) * 8 + lax.rem(my_z + 8 - dz, 8)

    def grp_offsets(t):
        a, n = 3 - (t - 1) // 4, lax.rem(t - 1, 4)
        return a, lax.rem(6 + (2 * lax.rem(n, 2) - 1) * ((n + 1) // 2), 4)

    def grp_at(a, dy):
        r = lax.rem(side + a // 2, 2) * 2 + lax.rem(core + lax.rem(a, 2), 2)
        return r * 4 + lax.rem(my_cplx + dy, 4)

    def grp_to(t):
        a, dy = grp_offsets(t)
        return grp_at(a, dy)

    def grp_from(t):
        a, dy = grp_offsets(t)
        return grp_at(a, 4 - dy)

    def row_id(d, h):
        return {"rep": side * 2 + h, "row": d}

    def grp_id(d):
        return {"rep": d // 4, "cplx": lax.rem(d, 4)}

    barrier = pltpu.get_barrier_semaphore()

    def greet_row(t, _):
        for h in range(2):
            pl.semaphore_signal(barrier, inc=1, device_id=row_id(row_to(t), h), device_id_type=MESH)
        return 0

    def greet_grp(t, _):
        pl.semaphore_signal(barrier, inc=1, device_id=grp_id(grp_to(t)), device_id_type=MESH)
        return 0

    mine, theirs = pl.ds(core * PART, PART), pl.ds(mate * PART, PART)
    loads = [
        pltpu.make_async_copy(a, b, isem.at[n])
        for n, (a, b) in enumerate((
            (pm_in.at[0, mine], pm.at[mine]), (w1_in, w1), (n1_in, n1), (mask_in, masks.at[core]),
            (f1_in, f1), (m1_in, m1), (w2_in, w2), (n2_in, n2),
            (f2_in, f2), (m2_in, m2), (ct_in.at[0, mine], ct.at[mine]),
        ))
    ]
    for load in loads:
        load.start()
    lax.fori_loop(1, ROWS, greet_row, 0)
    lax.fori_loop(1, groups, greet_grp, 0)

    def swap(n, src, dst):
        return pltpu.make_async_remote_copy(
            src_ref=src, dst_ref=dst, send_sem=xsem.at[n], recv_sem=ysem.at[n],
            device_id=row_id(me, mate), device_id_type=MESH)

    def row_copy(src, dst, phase, d, h, n, slot):
        return pltpu.make_async_remote_copy(
            src_ref=src, dst_ref=dst, send_sem=ssem.at[phase, n], recv_sem=rsem.at[phase, slot],
            device_id=row_id(d, h), device_id_type=MESH)

    def grp_copy(src, dst, phase, d, slot):
        return pltpu.make_async_remote_copy(
            src_ref=src, dst_ref=dst, send_sem=ssem.at[phase, d], recv_sem=rsem.at[phase, slot],
            device_id=grp_id(d), device_id_type=MESH)

    def lanes(i):
        return pl.ds(pl.multiple_of(i * TILE, TILE), TILE)

    def tiles(chain, body):
        def step(i, _):
            body(chain * PART + i, chain, i)
            return 0

        lax.fori_loop(0, PART, step, 0, unroll=4)

    def scatter(chain, stages, send, recv, phase):
        def fill(d, slot, ref):
            for n, stage in enumerate(stages):
                ref[slot, n * 32 : n * 32 + 32, :] = stage[
                    chain, pl.ds(pl.multiple_of(d * 32, 32), 32), :
                ].astype(BF16)

        def post(d):
            slot = chain * ROWS + d
            fill(d, slot, send)
            row_copy(send.at[slot], recv.at[core * ROWS + me], phase, d, chain, slot,
                     core * ROWS + me).start()

        def body(t, _):
            post(row_to(t))
            return 0

        lax.fori_loop(1, ROWS, body, 0)

        @pl.when(core == chain)
        def _():
            fill(me, core * ROWS + me, recv)

        @pl.when(core != chain)
        def _():
            post(me)

    def others(body):
        def step(t, _):
            d = row_to(t)
            body(d, 0)
            body(d, 1)
            return 0

        lax.fori_loop(1, ROWS, step, 0)
        body(me, mate)

    def give_back(send, recv, phase):
        def post(d, h):
            slot = h * ROWS + d
            row_copy(send.at[slot], recv.at[core * ROWS + me], phase, d, h, slot,
                     core * ROWS + me).start()

        others(post)
        recv[core * ROWS + me] = send[core * ROWS + me]

    def others_from(body):
        def step(t, _):
            s = row_from(t)
            body(s, 0)
            body(s, 1)
            return 0

        lax.fori_loop(1, ROWS, step, 0)
        body(me, mate)

    def gathered(recv, phase):
        def take(s, h):
            slot = h * ROWS + s
            row_copy(recv.at[slot], recv.at[slot], phase, s, h, slot, slot).wait_recv()

        others_from(take)

    def returned(chain, recv, phase, stages):
        def take(s):
            slot = chain * ROWS + s
            for n, stage in enumerate(stages):
                stage[chain, pl.ds(pl.multiple_of(s * 32, 32), 32), :] = recv[
                    slot, n * 32 : n * 32 + 32, :
                ].astype(F32)

        def wait(s):
            slot = chain * ROWS + s
            row_copy(recv.at[slot], recv.at[slot], phase, s, chain, slot, slot).wait_recv()

        @pl.when(core != chain)
        def _():
            wait(me)

        take(me)

        def body(t, _):
            s = row_from(t)
            wait(s)
            take(s)
            return 0

        lax.fori_loop(1, ROWS, body, 0)

    def sent(send, phase):
        def take(d, h):
            slot = h * ROWS + d
            row_copy(send.at[slot], send.at[slot], phase, d, h, slot, slot).wait_send()

        others(take)

    def left(chain, send, phase):
        def take(d):
            slot = chain * ROWS + d
            row_copy(send.at[slot], send.at[slot], phase, d, chain, slot, slot).wait_send()

        def body(t, _):
            take(row_to(t))
            return 0

        lax.fori_loop(1, ROWS, body, 0)

        @pl.when(core != chain)
        def _():
            take(me)

    def strided(i):
        return pl.ds(i, TILE, stride=PART)

    low = lax.rem(lax.broadcasted_iota(jnp.int32, (TILE, TILE), 0), 8) < 4

    def halves(a, b):
        return (
            jnp.where(low, a, pltpu.roll(b, 4, 0)),
            jnp.where(low, pltpu.roll(a, TILE - 4, 0), b),
        )

    def four_of(recv, base, q):
        block = recv[:, pl.ds(pl.multiple_of(base + 16 * q, 16), 16), :].astype(F32)
        result = []
        for n in range(2):
            part = block[:, 8 * n : 8 * n + 8, :]
            a, b = part[0:ROWS].reshape(TILE, TILE), part[ROWS:].reshape(TILE, TILE)
            result += [m.astype(BF16) for m in halves(a, b)]
        return result

    def put_four(send, base, q, four):
        first, second = halves(four[0], four[1]), halves(four[2], four[3])
        where = pl.ds(pl.multiple_of(base + 16 * q, 16), 16)
        for h in range(2):
            both = [m[h].reshape(ROWS, 8, TILE) for m in (first, second)]
            send[h * ROWS : h * ROWS + ROWS, where, :] = jnp.concatenate(both, axis=1).astype(BF16)

    def fours(body):
        def step(q, _):
            body(q)
            return 0

        lax.fori_loop(0, 2, step, 0)

    def forward_channels(u, recv, send):
        def body(q):
            left, right = four_of(recv, 0, q), four_of(recv, 32, q)
            result = []
            for n in range(4):
                ch_l[u, 4 * q + n] = left[n]
                ch_r[u, 4 * q + n] = right[n]
                result.append(nt(left[n], right[n]) if u == 0 else tn(left[n], right[n]))
            put_four(send, 0, q, result)

        fours(body)

    def backward_channels(u, recv, send):
        def body(q):
            grads = four_of(recv, 0, q)
            lefts, rights = [], []
            for n in range(4):
                left, right, grad = ch_l[u, 4 * q + n], ch_r[u, 4 * q + n], grads[n]
                if u == 0:
                    lefts.append(nn(grad, right))
                    rights.append(tn(grad, left))
                else:
                    lefts.append(nt(right, grad))
                    rights.append(nn(left, grad))
            put_four(send, 0, q, lefts)
            put_four(send, 32, q, rights)

        fours(body)

    def front(u, i, chain, part, x):
        standard, inv_std = normalize(x)
        std[u, i] = standard
        inv[u, i] = inv_std
        normed = (standard * ngain[u]).astype(BF16)
        nrm[u, :, lanes(i)] = normed
        projected = nn(wt[u], normed)
        pair_mask = rowm[i] * masks[chain].astype(F32)
        s = jax.nn.sigmoid(projected[0:128])
        left = s * projected[128:256] * pair_mask
        cf[u, 0, i] = left * (1.0 - s)
        cf[u, 1, i] = s * pair_mask
        s_a[chain, strided(part), :] = left
        t = jax.nn.sigmoid(projected[256:384])
        right = t * projected[384:512] * pair_mask
        cf[u, 2, i] = right * (1.0 - t)
        cf[u, 3, i] = t * pair_mask
        s_b[chain, strided(part), :] = right
        gate[u, i] = jax.nn.sigmoid(projected[512:640])

    def finish(u, i, chain, part):
        prod_hat, mid_inv = normalize(s_a[chain, strided(part), :])
        middle = (prod_hat * mgain[u]).astype(BF16)
        update = nn(ft[u], middle)
        ph[u, i] = prod_hat
        minv[u, i] = mid_inv
        mdl[u, :, lanes(i)] = middle
        upd[u, i] = update
        return update, prod_hat, mid_inv

    def upper(u, i, chain, part, incoming, update, prod_hat, mid_inv, final):
        g = gate[u, i]
        inc[u, i] = incoming
        grad_update = (g * incoming).astype(BF16)
        gup[u, :, lanes(i)] = grad_update
        gproj[u, 512:640, lanes(i)] = (incoming * update * g * (1.0 - g)).astype(BF16)
        grad_middle = nn(final[...], grad_update)
        macc[u] += grad_middle * prod_hat
        s_b[chain, strided(part), :] = norm_back(grad_middle * mgain[u], prod_hat, mid_inv)

    def lower(u, i, chain, part, weight):
        grad_left, grad_right = s_a[chain, strided(part), :], s_b[chain, strided(part), :]
        gproj[u, 0:128, lanes(i)] = (grad_left * cf[u, 0, i]).astype(BF16)
        gproj[u, 128:256, lanes(i)] = (grad_left * cf[u, 1, i]).astype(BF16)
        gproj[u, 256:384, lanes(i)] = (grad_right * cf[u, 2, i]).astype(BF16)
        gproj[u, 384:512, lanes(i)] = (grad_right * cf[u, 3, i]).astype(BF16)
        grad_normed = nn(weight[...], gproj[u, :, lanes(i)])
        standard = std[u, i]
        gacc[u] += grad_normed * standard
        back = norm_back(grad_normed * ngain[u], standard, inv[u, i])
        return (inc[u, i] + back).astype(BF16)

    def spread(row):
        return jnp.broadcast_to(row[...], (TILE, TILE)).T

    def weights(u, w, n):
        for g in range(5):
            wt[u, g * 128 : g * 128 + 128, :] = turn(w[:, g * 128 : g * 128 + 128])
        ngain[u] = spread(n)

    for load in loads[0:4]:
        load.wait()
    weights(0, w1, n1)
    where = lax.broadcasted_iota(jnp.int32, (1, TILE), 1)

    def row_masks(chain):
        col_mask = masks[chain].astype(F32)
        for i in range(PART):
            here = where == me * OWN + core * PART + i
            picked = jnp.sum(jnp.where(here, col_mask, 0.0), axis=1, keepdims=True)
            rowm[chain * PART + i] = jnp.broadcast_to(picked, (1, TILE))

    row_masks(core)
    pl.semaphore_wait(barrier, 2 * (ROWS - 1) + groups - 1)
    swaps = [
        swap(0, pm_in.at[0, theirs], pm.at[mine]),
        swap(1, mask_in, masks.at[core]),
        swap(2, ct_in.at[0, theirs], ct.at[mine]),
    ]
    for copy in swaps:
        copy.start()

    def first(i, chain, part):
        x = pm[i].astype(F32).T
        xt[i] = x
        front(0, i, chain, part, x)

    def scatter_first(chain):
        scatter(chain, (s_a, s_b), send2.at[0], recv2.at[0], 0)

    tiles(core, first)

    @pl.when(core == 0)
    def _():
        scatter_first(0)

    swaps[0].wait()
    swaps[1].wait()
    row_masks(mate)
    tiles(mate, first)

    @pl.when(core == 1)
    def _():
        scatter_first(0)

    left(0, send2.at[0], 0)
    scatter_first(1)
    for load in loads[4:]:
        load.wait()
    swaps[2].wait()
    weights(1, w2, n2)
    for u, (f, m) in enumerate(((f1, m1), (f2, m2))):
        ft[u] = turn(f[...])
        mgain[u] = spread(m)
        gacc[u] = jnp.zeros((TILE, TILE), F32)
        macc[u] = jnp.zeros((TILE, TILE), F32)
    gathered(recv2.at[0], 0)
    forward_channels(0, recv2.at[0], send1.at[0])
    give_back(send1.at[0], recv1.at[0], 1)
    left(1, send2.at[0], 0)

    def second(i, chain, part):
        update, _, _ = finish(0, i, chain, part)
        first_out = (xt[i] + gate[0, i] * update).astype(BF16)
        front(1, i, chain, part, first_out.astype(F32))

    for chain in range(2):
        returned(chain, recv1.at[0], 1, (s_a,))
        tiles(chain, second)
        if chain == 1:
            left(0, send2.at[1], 2)
        scatter(chain, (s_a, s_b), send2.at[1], recv2.at[1], 2)
    sent(send1.at[0], 1)
    gathered(recv2.at[1], 2)
    forward_channels(1, recv2.at[1], send1.at[1])
    give_back(send1.at[1], recv1.at[1], 3)
    left(1, send2.at[1], 2)

    def third(i, chain, part):
        update, prod_hat, mid_inv = finish(1, i, chain, part)
        upper(1, i, chain, part, ct[i].astype(F32).T, update, prod_hat, mid_inv, f2)

    for chain in range(2):
        returned(chain, recv1.at[1], 3, (s_a,))
        tiles(chain, third)
        if chain == 1:
            left(0, send1.at[2], 4)
        scatter(chain, (s_b,), send1.at[2], recv1.at[2], 4)
    sent(send1.at[1], 3)
    pay[640:768, :] = nt(mdl[1], gup[1])
    gathered(recv1.at[2], 4)
    backward_channels(1, recv1.at[2], send2.at[2])
    give_back(send2.at[2], recv2.at[2], 5)
    left(1, send1.at[2], 4)

    def fourth(i, chain, part):
        first_grad = lower(1, i, chain, part, w2).astype(F32)
        upper(0, i, chain, part, first_grad, upd[0, i], ph[0, i], minv[0, i], f1)

    for chain in range(2):
        returned(chain, recv2.at[2], 5, (s_a, s_b))
        tiles(chain, fourth)
        if chain == 1:
            left(0, send1.at[3], 6)
        scatter(chain, (s_b,), send1.at[3], recv1.at[3], 6)
    sent(send2.at[2], 5)

    def vectors(values):
        vec[...] = jnp.zeros(vec.shape, F32)
        for n, value in enumerate(values):
            vec[n : n + 1, :] = jnp.sum(value.T, axis=0, keepdims=True)

    def blocks_out(send, recv, phase, block):
        def fill(d, ref):
            ref[d, 0:block, :] = pay[pl.ds(pl.multiple_of(d * block, block), block), :].astype(BF16)
            ref[d, block : block + 16, :] = vec[...].astype(BF16)

        fill(mq, recv)

        def body(t, _):
            d = grp_to(t)
            fill(d, send)
            grp_copy(send.at[d], recv.at[mq], phase, d, mq).start()
            return 0

        lax.fori_loop(1, groups, body, 0)

    def blocks_in(send, recv, phase):
        def body(t, _):
            s = grp_from(t)
            grp_copy(send.at[s], recv.at[s], phase, s, s).wait()
            return 0

        lax.fori_loop(1, groups, body, 0)
        return jnp.sum(recv[...].astype(F32), axis=0)

    def whole_out(value, send, recv, phase):
        send[...] = value.astype(BF16)
        recv[me] = value.astype(BF16)

        def body(t, _):
            d = row_to(t)
            row_copy(send, recv.at[me], phase, d, core, d, me).start()
            return 0

        lax.fori_loop(1, ROWS, body, 0)

    def whole_in(send, recv, phase):
        def body(t, _):
            s = row_from(t)
            row_copy(send, recv.at[s], phase, s, core, s, s).wait()
            return 0

        lax.fori_loop(1, ROWS, body, 0)
        return jnp.sum(recv[...].astype(F32), axis=0)

    def back_out(value, send, recv, phase):
        send[...] = value.astype(BF16)
        recv[mq] = value.astype(BF16)

        def body(t, _):
            d = grp_to(t)
            grp_copy(send, recv.at[mq], phase, d, mq).start()
            return 0

        lax.fori_loop(1, groups, body, 0)

    def back_in(send, recv, phase):
        def body(t, _):
            s = grp_from(t)
            grp_copy(send, recv.at[s], phase, s, s).wait()
            return 0

        lax.fori_loop(1, groups, body, 0)

    proj = nt(nrm[1], gproj[1])
    for g in range(5):
        pay[g * 128 : g * 128 + 128, :] = proj[:, g * 128 : g * 128 + 128]
    pay[768:896, :] = nt(mdl[0], gup[0])
    pay[896:1024, :] = nt(nrm[0], gproj[0, 512:640, :])
    vectors((gacc[1], macc[1], macc[0]))
    blocks_out(a2s, a2r, 8, 64)

    gathered(recv1.at[3], 6)
    backward_channels(0, recv1.at[3], send2.at[3])
    give_back(send2.at[3], recv2.at[3], 7)
    left(1, send1.at[3], 6)
    whole_out(blocks_in(a2s, a2r, 8), b2s, b2r, 9)

    def fifth(i, chain, part):
        out[i] = lower(0, i, chain, part, w1).astype(F32).T.astype(BF16)

    for chain in range(2):
        returned(chain, recv2.at[3], 7, (s_a, s_b))
        tiles(chain, fifth)
    sent(send2.at[3], 7)
    stores = [pltpu.make_async_copy(out.at[mine], out_to.at[0, mine], osem.at[0])]
    stores[0].start()
    swap_back = swap(3, out.at[theirs], out_to.at[0, mine])
    swap_back.start()

    def store(n, a, b):
        stores.append(pltpu.make_async_copy(a, b, osem.at[n]))
        stores[-1].start()

    proj = nt(nrm[0], gproj[0, 0:512, :])
    for g in range(4):
        pay[g * 128 : g * 128 + 128, :] = proj[:, g * 128 : g * 128 + 128]
    vectors((gacc[0],))
    blocks_out(a1s, a1r, 11, 32)

    total = whole_in(b2s, b2r, 9)
    back_out(total[0:64], c2s, c2r, 10)
    o_n2[...] = total[64:65] * factor
    o_m2[...] = total[65:66] * factor
    o_m1[...] = total[66:67] * factor
    store(1, o_n2, n2_to)
    store(2, o_m2, m2_to)
    store(3, o_m1, m1_to)

    whole_out(blocks_in(a1s, a1r, 11), b1s, b1r, 12)
    back_in(c2s, c2r, 10)
    sums = c2r[...].reshape(1024, TILE).astype(F32) * factor
    for g in range(5):
        o_p2[:, g * 128 : g * 128 + 128] = sums[g * 128 : g * 128 + 128]
    o_f2[...] = sums[640:768]
    o_f1[...] = sums[768:896]
    o_p1[:, 512:640] = sums[896:1024]
    store(4, o_p2, p2_to)
    store(5, o_f2, f2_to)
    store(6, o_f1, f1_to)

    total = whole_in(b1s, b1r, 12)
    back_out(total[0:32], c1s, c1r, 13)
    o_n1[...] = total[32:33] * factor
    store(7, o_n1, n1_to)
    back_in(c1s, c1r, 13)
    sums = c1r[...].reshape(512, TILE).astype(F32) * factor
    for g in range(4):
        o_p1[:, g * 128 : g * 128 + 128] = sums[g * 128 : g * 128 + 128]

    store(8, o_p1, p1_to)
    for copy in stores:
        copy.wait()
    swap_back.wait()


def hand_on(*refs):
    froms, tos, held, sems = refs[:9], refs[9:18], refs[18:27], refs[27]
    loads = [pltpu.make_async_copy(a, b, sems.at[0, n]) for n, (a, b) in enumerate(zip(froms, held))]
    stores = [pltpu.make_async_copy(a, b, sems.at[1, n]) for n, (a, b) in enumerate(zip(held, tos))]
    for load in loads:
        load.start()
    for load, store in zip(loads, stores):
        load.wait()
        store.start()
    for store in stores:
        store.wait()


def on_device(groups, factor, pm, ct, mask, n1, w1, m1, f1, n2, w2, m2, f2):
    wide = (1, TILE)
    shapes = [
        (pm.shape, BF16),
        (wide, F32), ((TILE, 640), F32), (wide, F32), ((TILE, TILE), F32),
        (wide, F32), ((TILE, 640), F32), (wide, F32), ((TILE, TILE), F32),
    ]
    tile = (OWN, TILE, TILE)
    lane = (TILE, OWN * TILE)
    loaded = [
        (pm.shape[1:], BF16), (ct.shape[1:], BF16), ((2,) + mask.shape, jnp.int32),
        (wide, F32), ((TILE, 640), BF16), (wide, F32), ((TILE, TILE), BF16),
        (wide, F32), ((TILE, 640), BF16), (wide, F32), ((TILE, TILE), BF16),
    ]
    scratch = [pltpu.VMEM(s, d) for s, d in loaded + [(pm.shape[1:], BF16)] + shapes[1:]] + [
        pltpu.VMEM((2, 640, TILE), BF16),
        pltpu.VMEM((2, TILE, TILE), BF16),
        pltpu.VMEM((2, TILE, TILE), F32),
        pltpu.VMEM((2, TILE, TILE), F32),
        pltpu.VMEM((OWN, 1, TILE), F32),
        pltpu.VMEM(tile, F32),
        pltpu.VMEM((2,) + tile, F32),
        pltpu.VMEM((2, OWN, 1, TILE), F32),
        pltpu.VMEM((2,) + lane, BF16),
        pltpu.VMEM((2, 4) + tile, F32),
        pltpu.VMEM((2,) + tile, F32),
        pltpu.VMEM((2,) + tile, F32),
        pltpu.VMEM((2, OWN, 1, TILE), F32),
        pltpu.VMEM((2,) + lane, BF16),
        pltpu.VMEM((2,) + tile, F32),
        pltpu.VMEM((2,) + lane, BF16),
        pltpu.VMEM((2, 640, OWN * TILE), BF16),
        pltpu.VMEM((2,) + tile, F32),
        pltpu.VMEM((2, PART * TILE, TILE), F32),
        pltpu.VMEM((2, PART * TILE, TILE), F32),
        pltpu.VMEM((2,) + tile, BF16),
        pltpu.VMEM((2,) + tile, BF16),
        pltpu.VMEM((2, TILE, TILE), F32),
        pltpu.VMEM((2, TILE, TILE), F32),
        pltpu.VMEM((1024, TILE), F32),
        pltpu.VMEM((16, TILE), F32),
        pltpu.VMEM((4, 2 * ROWS, 64, TILE), BF16),
        pltpu.VMEM((4, 2 * ROWS, 64, TILE), BF16),
        pltpu.VMEM((4, 2 * ROWS, 32, TILE), BF16),
        pltpu.VMEM((4, 2 * ROWS, 32, TILE), BF16),
        pltpu.VMEM((16, 80, TILE), BF16),
        pltpu.VMEM((16, 80, TILE), BF16),
        pltpu.VMEM((80, TILE), BF16),
        pltpu.VMEM((ROWS, 80, TILE), BF16),
        pltpu.VMEM((64, TILE), BF16),
        pltpu.VMEM((16, 64, TILE), BF16),
        pltpu.VMEM((16, 48, TILE), BF16),
        pltpu.VMEM((16, 48, TILE), BF16),
        pltpu.VMEM((48, TILE), BF16),
        pltpu.VMEM((ROWS, 48, TILE), BF16),
        pltpu.VMEM((32, TILE), BF16),
        pltpu.VMEM((16, 32, TILE), BF16),
        pltpu.SemaphoreType.DMA((14, 2 * ROWS)),
        pltpu.SemaphoreType.DMA((14, 2 * ROWS)),
        pltpu.SemaphoreType.DMA((11,)),
        pltpu.SemaphoreType.DMA((9,)),
        pltpu.SemaphoreType.DMA((4,)),
        pltpu.SemaphoreType.DMA((4,)),
    ]
    anywhere = pl.BlockSpec(memory_space=pl.ANY)
    results = pl.pallas_call(
        functools.partial(kernel, groups, factor),
        out_shape=[jax.ShapeDtypeStruct(s, d) for s, d in shapes],
        in_specs=[anywhere] * 11,
        out_specs=[anywhere] * 9,
        scratch_shapes=scratch,
        compiler_params=pltpu.CompilerParams(
            collective_id=0, has_side_effects=True, vmem_limit_bytes=VMEM_BYTES
        ),
        name="triangle",
    )(
        pm, ct, mask,
        n1.reshape(wide), w1, m1.reshape(wide), f1,
        n2.reshape(wide), w2, m2.reshape(wide), f2,
    )
    results = pl.pallas_call(
        hand_on,
        out_shape=[jax.ShapeDtypeStruct(s, d) for s, d in shapes],
        in_specs=[anywhere] * 9,
        out_specs=[anywhere] * 9,
        scratch_shapes=[pltpu.VMEM(s, d) for s, d in shapes] + [pltpu.SemaphoreType.DMA((2, 9))],
        compiler_params=pltpu.CompilerParams(vmem_limit_bytes=VMEM_BYTES),
        name="hand_on",
    )(*results)
    flat = [r.reshape(TILE) if r.shape == wide else r for r in results]
    return tuple(flat)


def solution(mesh):
    groups = mesh.shape["rep"] * mesh.shape["cplx"]
    factor = 1.0 / math.sqrt(groups * TILE * TILE)
    blocks = P(("rep", "cplx"), "row", None, None)
    placed = (blocks, blocks, P(("rep", "cplx"), None)) + (P(),) * 8
    return jax.shard_map(
        functools.partial(on_device, groups, factor),
        mesh=mesh,
        in_specs=placed,
        out_specs=(blocks,) + (P(),) * 8,
        check_vma=False,
    )
```

```python
import functools
import math

import jax
import jax.numpy as jnp
from jax import lax
from jax.experimental import pallas as pl
from jax.experimental.pallas import tpu as pltpu
from jax.sharding import PartitionSpec as P

EPS = 1e-05
MESH = pl.DeviceIdType.MESH
F32 = jnp.float32
BF16 = jnp.bfloat16
ROWS = 16
TILE = 128
VMEM_BYTES = 63 * 1024 * 1024
OWN = 8
PART = 4


def nn(a, b):
    return lax.dot_general(a, b, (((1,), (0,)), ((), ())), preferred_element_type=F32)


def nt(a, b):
    return lax.dot_general(a, b, (((1,), (1,)), ((), ())), preferred_element_type=F32)


def turn(a):
    return a.astype(F32).T.astype(BF16)


def tn(a, b):
    return nn(turn(a), b)


def mean0(a):
    return jnp.mean(a, axis=0, keepdims=True)


def normalize(a):
    centered = a - mean0(a)
    inv = lax.rsqrt(mean0(centered * centered) + EPS)
    return centered * inv, inv


def norm_back(e, standard, inv):
    return inv * (e - mean0(e) - standard * mean0(e * standard))


def kernel(
    groups, factor,
    pm_in, ct_in, mask_in, n1_in, w1_in, m1_in, f1_in, n2_in, w2_in, m2_in, f2_in,
    out_to, n1_to, p1_to, m1_to, f1_to, n2_to, p2_to, m2_to, f2_to,
    pm, ct, masks, n1, w1, m1, f1, n2, w2, m2, f2,
    out, o_n1, o_p1, o_m1, o_f1, o_n2, o_p2, o_m2, o_f2,
    wt, ft, ngain, mgain, rowm,
    xt, std, inv, nrm, cf, gate, ph, minv, mdl, upd, gup, gproj, inc,
    s_a, s_b, ch_l, ch_r,
    gacc, macc, pay, vec,
    send2, recv2, send1, recv1,
    a2s, a2r, b2s, b2r, c2s, c2r, a1s, a1r, b1s, b1r, c1s, c1r,
    ssem, rsem, gssem, grsem, isem, osem, xsem, ysem,
):
    me = lax.axis_index("row")
    my_x, my_z = me // 8, lax.rem(me, 8)
    my_rep, my_cplx = lax.axis_index("rep"), lax.axis_index("cplx")
    side, core = my_rep // 2, lax.rem(my_rep, 2)
    mate = 1 - core
    mq = my_rep * 4 + my_cplx

    def offsets(t):
        n = lax.rem(t - 1, 8)
        return 1 - (t - 1) // 8, lax.rem(12 + (2 * lax.rem(n, 2) - 1) * ((n + 1) // 2), 8)

    def row_to(t):
        dx, dz = offsets(t)
        return lax.rem(my_x + dx, 2) * 8 + lax.rem(my_z + dz, 8)

    def row_from(t):
        dx, dz = offsets(t)
        return lax.rem(my_x + dx, 2) * 8 + lax.rem(my_z + 8 - dz, 8)

    def grp_offsets(t):
        a, n = 3 - (t - 1) // 4, lax.rem(t - 1, 4)
        return a, lax.rem(6 + (2 * lax.rem(n, 2) - 1) * ((n + 1) // 2), 4)

    def grp_at(a, dy):
        r = lax.rem(side + a // 2, 2) * 2 + lax.rem(core + lax.rem(a, 2), 2)
        return r * 4 + lax.rem(my_cplx + dy, 4)

    def grp_to(t):
        a, dy = grp_offsets(t)
        return grp_at(a, dy)

    def grp_from(t):
        a, dy = grp_offsets(t)
        return grp_at(a, 4 - dy)

    def row_id(d, h):
        return {"rep": side * 2 + h, "row": d}

    def grp_id(d):
        return {"rep": d // 4, "cplx": lax.rem(d, 4)}

    barrier = pltpu.get_barrier_semaphore()

    def greet_row(t, _):
        for h in range(2):
            pl.semaphore_signal(barrier, inc=1, device_id=row_id(row_to(t), h), device_id_type=MESH)
        return 0

    def greet_grp(t, _):
        pl.semaphore_signal(barrier, inc=1, device_id=grp_id(grp_to(t)), device_id_type=MESH)
        return 0

    mine, theirs = pl.ds(core * PART, PART), pl.ds(mate * PART, PART)
    loads = [
        pltpu.make_async_copy(a, b, isem.at[n])
        for n, (a, b) in enumerate((
            (pm_in.at[0, mine], pm.at[mine]), (w1_in, w1), (n1_in, n1), (mask_in, masks.at[core]),
            (f1_in, f1), (m1_in, m1), (w2_in, w2), (n2_in, n2),
            (f2_in, f2), (m2_in, m2), (ct_in.at[0, mine], ct.at[mine]),
        ))
    ]
    for load in loads:
        load.start()
    lax.fori_loop(1, ROWS, greet_row, 0)
    lax.fori_loop(1, groups, greet_grp, 0)

    def swap(n, src, dst):
        return pltpu.make_async_remote_copy(
            src_ref=src, dst_ref=dst, send_sem=xsem.at[n], recv_sem=ysem.at[n],
            device_id=row_id(me, mate), device_id_type=MESH)

    def row_copy(src, dst, send_sem, recv_sem, d, h):
        return pltpu.make_async_remote_copy(
            src_ref=src, dst_ref=dst, send_sem=send_sem, recv_sem=recv_sem,
            device_id=row_id(d, h), device_id_type=MESH)

    def grp_copy(src, dst, send_sem, recv_sem, d):
        return pltpu.make_async_remote_copy(
            src_ref=src, dst_ref=dst, send_sem=send_sem, recv_sem=recv_sem,
            device_id=grp_id(d), device_id_type=MESH)

    def bytes_of(ref, sem):
        pltpu.make_async_copy(ref, ref, sem).wait()

    def lanes(i):
        return pl.ds(pl.multiple_of(i * TILE, TILE), TILE)

    def tiles(chain, body):
        def step(i, _):
            body(chain * PART + i, chain, i)
            return 0

        lax.fori_loop(0, PART, step, 0, unroll=4)

    def scatter(chain, stages, send, recv, phase):
        base = chain * ROWS
        mine_there = core * ROWS + me
        for n, stage in enumerate(stages):
            whole = stage[chain].reshape(ROWS, 32, TILE).astype(BF16)
            send[pl.ds(base, ROWS), n * 32 : n * 32 + 32, :] = whole

        def post(d):
            row_copy(send.at[base + d], recv.at[mine_there], ssem.at[phase, chain],
                     rsem.at[phase, 0], d, chain).start()

        def body(t, _):
            post(row_to(t))
            return 0

        lax.fori_loop(1, ROWS, body, 0)

        @pl.when(core == chain)
        def _():
            recv[mine_there] = send[base + me]

        @pl.when(core != chain)
        def _():
            post(me)

    def left(chain, send, phase):
        @pl.when(core == chain)
        def _():
            bytes_of(send.at[0 : ROWS - 1], ssem.at[phase, chain])

        @pl.when(core != chain)
        def _():
            bytes_of(send.at[0:ROWS], ssem.at[phase, chain])

    def give_back(send, recv, phase):
        mine_there = core * ROWS + me

        def post(d, h):
            column = core * 2 + lax.rem(d // 8 + my_x, 2)
            row_copy(send.at[h * ROWS + d], recv.at[mine_there], ssem.at[phase, 0],
                     rsem.at[phase, column], d, h).start()

        def body(t, _):
            d = row_to(t)
            post(d, 0)
            post(d, 1)
            return 0

        lax.fori_loop(1, ROWS, body, 0)
        post(me, mate)
        recv[mine_there] = send[mine_there]

    def gave(send, phase):
        bytes_of(send.at[0 : 2 * ROWS - 1], ssem.at[phase, 0])

    def gathered(recv, phase):
        bytes_of(recv.at[0 : 2 * ROWS - 1], rsem.at[phase, 0])

    def returned(chain, recv, phase, stages):
        def take(x):
            slots = pl.ds(chain * ROWS + x * 8, 8)
            rows = pl.ds(pl.multiple_of(x * 256, 256), 256)
            for n, stage in enumerate(stages):
                block = recv[slots, n * 32 : n * 32 + 32, :].astype(F32)
                stage[chain, rows, :] = block.reshape(256, TILE)

        bytes_of(recv.at[0:8], rsem.at[phase, chain * 2 + 1])
        take(1 - my_x)

        @pl.when(core == chain)
        def _():
            bytes_of(recv.at[0:7], rsem.at[phase, chain * 2])

        @pl.when(core != chain)
        def _():
            bytes_of(recv.at[0:8], rsem.at[phase, chain * 2])

        take(my_x)

    def strided(i):
        return pl.ds(i, TILE, stride=PART)

    low = lax.rem(lax.broadcasted_iota(jnp.int32, (TILE, TILE), 0), 8) < 4

    def halves(a, b):
        return (
            jnp.where(low, a, pltpu.roll(b, 4, 0)),
            jnp.where(low, pltpu.roll(a, TILE - 4, 0), b),
        )

    def four_of(recv, base, q):
        block = recv[:, pl.ds(pl.multiple_of(base + 16 * q, 16), 16), :].astype(F32)
        result = []
        for n in range(2):
            part = block[:, 8 * n : 8 * n + 8, :]
            a, b = part[0:ROWS].reshape(TILE, TILE), part[ROWS:].reshape(TILE, TILE)
            result += [m.astype(BF16) for m in halves(a, b)]
        return result

    def put_four(send, base, q, four):
        first, second = halves(four[0], four[1]), halves(four[2], four[3])
        where = pl.ds(pl.multiple_of(base + 16 * q, 16), 16)
        for h in range(2):
            both = [m[h].reshape(ROWS, 8, TILE) for m in (first, second)]
            send[h * ROWS : h * ROWS + ROWS, where, :] = jnp.concatenate(both, axis=1).astype(BF16)

    def fours(body):
        def step(q, _):
            body(q)
            return 0

        lax.fori_loop(0, 2, step, 0)

    def forward_channels(u, recv, send):
        def body(q):
            left, right = four_of(recv, 0, q), four_of(recv, 32, q)
            result = []
            for n in range(4):
                ch_l[u, 4 * q + n] = left[n]
                ch_r[u, 4 * q + n] = right[n]
                result.append(nt(left[n], right[n]) if u == 0 else tn(left[n], right[n]))
            put_four(send, 0, q, result)

        fours(body)

    def backward_channels(u, recv, send):
        def body(q):
            grads = four_of(recv, 0, q)
            lefts, rights = [], []
            for n in range(4):
                left, right, grad = ch_l[u, 4 * q + n], ch_r[u, 4 * q + n], grads[n]
                if u == 0:
                    lefts.append(nn(grad, right))
                    rights.append(tn(grad, left))
                else:
                    lefts.append(nt(right, grad))
                    rights.append(nn(left, grad))
            put_four(send, 0, q, lefts)
            put_four(send, 32, q, rights)

        fours(body)

    def front(u, i, chain, part, x):
        standard, inv_std = normalize(x)
        std[u, i] = standard
        inv[u, i] = inv_std
        normed = (standard * ngain[u]).astype(BF16)
        nrm[u, :, lanes(i)] = normed
        projected = nn(wt[u], normed)
        pair_mask = rowm[i] * masks[chain].astype(F32)
        s = jax.nn.sigmoid(projected[0:128])
        left = s * projected[128:256] * pair_mask
        cf[u, 0, i] = left * (1.0 - s)
        cf[u, 1, i] = s * pair_mask
        s_a[chain, strided(part), :] = left
        t = jax.nn.sigmoid(projected[256:384])
        right = t * projected[384:512] * pair_mask
        cf[u, 2, i] = right * (1.0 - t)
        cf[u, 3, i] = t * pair_mask
        s_b[chain, strided(part), :] = right
        gate[u, i] = jax.nn.sigmoid(projected[512:640])

    def finish(u, i, chain, part):
        prod_hat, mid_inv = normalize(s_a[chain, strided(part), :])
        middle = (prod_hat * mgain[u]).astype(BF16)
        update = nn(ft[u], middle)
        ph[u, i] = prod_hat
        minv[u, i] = mid_inv
        mdl[u, :, lanes(i)] = middle
        upd[u, i] = update
        return update, prod_hat, mid_inv

    def upper(u, i, chain, part, incoming, update, prod_hat, mid_inv, final):
        g = gate[u, i]
        inc[u, i] = incoming
        grad_update = (g * incoming).astype(BF16)
        gup[u, :, lanes(i)] = grad_update
        gproj[u, 512:640, lanes(i)] = (incoming * update * g * (1.0 - g)).astype(BF16)
        grad_middle = nn(final[...], grad_update)
        macc[u] += grad_middle * prod_hat
        s_b[chain, strided(part), :] = norm_back(grad_middle * mgain[u], prod_hat, mid_inv)

    def lower(u, i, chain, part, weight):
        grad_left, grad_right = s_a[chain, strided(part), :], s_b[chain, strided(part), :]
        gproj[u, 0:128, lanes(i)] = (grad_left * cf[u, 0, i]).astype(BF16)
        gproj[u, 128:256, lanes(i)] = (grad_left * cf[u, 1, i]).astype(BF16)
        gproj[u, 256:384, lanes(i)] = (grad_right * cf[u, 2, i]).astype(BF16)
        gproj[u, 384:512, lanes(i)] = (grad_right * cf[u, 3, i]).astype(BF16)
        grad_normed = nn(weight[...], gproj[u, :, lanes(i)])
        standard = std[u, i]
        gacc[u] += grad_normed * standard
        back = norm_back(grad_normed * ngain[u], standard, inv[u, i])
        return (inc[u, i] + back).astype(BF16)

    def spread(row):
        return jnp.broadcast_to(row[...], (TILE, TILE)).T

    def weights(u, w, n):
        for g in range(5):
            wt[u, g * 128 : g * 128 + 128, :] = turn(w[:, g * 128 : g * 128 + 128])
        ngain[u] = spread(n)

    for load in loads[0:4]:
        load.wait()
    weights(0, w1, n1)
    where = lax.broadcasted_iota(jnp.int32, (1, TILE), 1)

    def row_masks(chain):
        col_mask = masks[chain].astype(F32)
        for i in range(PART):
            here = where == me * OWN + core * PART + i
            picked = jnp.sum(jnp.where(here, col_mask, 0.0), axis=1, keepdims=True)
            rowm[chain * PART + i] = jnp.broadcast_to(picked, (1, TILE))

    row_masks(core)
    pl.semaphore_wait(barrier, 2 * (ROWS - 1) + groups - 1)
    swaps = [
        swap(0, pm_in.at[0, theirs], pm.at[mine]),
        swap(1, mask_in, masks.at[core]),
        swap(2, ct_in.at[0, theirs], ct.at[mine]),
    ]
    for copy in swaps:
        copy.start()

    def first(i, chain, part):
        x = pm[i].astype(F32).T
        xt[i] = x
        front(0, i, chain, part, x)

    def scatter_first(chain):
        scatter(chain, (s_a, s_b), send2.at[0], recv2.at[0], 0)

    tiles(core, first)

    @pl.when(core == 0)
    def _():
        scatter_first(0)

    swaps[0].wait()
    swaps[1].wait()
    row_masks(mate)
    tiles(mate, first)

    @pl.when(core == 1)
    def _():
        scatter_first(0)

    left(0, send2.at[0], 0)
    scatter_first(1)
    for load in loads[4:]:
        load.wait()
    swaps[2].wait()
    weights(1, w2, n2)
    for u, (f, m) in enumerate(((f1, m1), (f2, m2))):
        ft[u] = turn(f[...])
        mgain[u] = spread(m)
        gacc[u] = jnp.zeros((TILE, TILE), F32)
        macc[u] = jnp.zeros((TILE, TILE), F32)
    gathered(recv2.at[0], 0)
    forward_channels(0, recv2.at[0], send1.at[0])
    give_back(send1.at[0], recv1.at[0], 1)
    left(1, send2.at[0], 0)

    def second(i, chain, part):
        update, _, _ = finish(0, i, chain, part)
        first_out = (xt[i] + gate[0, i] * update).astype(BF16)
        front(1, i, chain, part, first_out.astype(F32))

    for chain in range(2):
        returned(chain, recv1.at[0], 1, (s_a,))
        tiles(chain, second)
        if chain == 1:
            left(0, send2.at[1], 2)
        scatter(chain, (s_a, s_b), send2.at[1], recv2.at[1], 2)
    gave(send1.at[0], 1)
    gathered(recv2.at[1], 2)
    forward_channels(1, recv2.at[1], send1.at[1])
    give_back(send1.at[1], recv1.at[1], 3)
    left(1, send2.at[1], 2)

    def third(i, chain, part):
        update, prod_hat, mid_inv = finish(1, i, chain, part)
        upper(1, i, chain, part, ct[i].astype(F32).T, update, prod_hat, mid_inv, f2)

    for chain in range(2):
        returned(chain, recv1.at[1], 3, (s_a,))
        tiles(chain, third)
        if chain == 1:
            left(0, send1.at[2], 4)
        scatter(chain, (s_b,), send1.at[2], recv1.at[2], 4)
    gave(send1.at[1], 3)
    pay[640:768, :] = nt(mdl[1], gup[1])
    gathered(recv1.at[2], 4)
    backward_channels(1, recv1.at[2], send2.at[2])
    give_back(send2.at[2], recv2.at[2], 5)
    left(1, send1.at[2], 4)

    def fourth(i, chain, part):
        first_grad = lower(1, i, chain, part, w2).astype(F32)
        upper(0, i, chain, part, first_grad, upd[0, i], ph[0, i], minv[0, i], f1)

    for chain in range(2):
        returned(chain, recv2.at[2], 5, (s_a, s_b))
        tiles(chain, fourth)
        if chain == 1:
            left(0, send1.at[3], 6)
        scatter(chain, (s_b,), send1.at[3], recv1.at[3], 6)
    gave(send2.at[2], 5)

    def vectors(values):
        vec[...] = jnp.zeros(vec.shape, F32)
        for n, value in enumerate(values):
            vec[n : n + 1, :] = jnp.sum(value.T, axis=0, keepdims=True)

    def blocks_out(send, recv, phase, block):
        def fill(d, ref):
            ref[d, 0:block, :] = pay[pl.ds(pl.multiple_of(d * block, block), block), :].astype(BF16)
            ref[d, block : block + 16, :] = vec[...].astype(BF16)

        fill(mq, recv)

        def body(t, _):
            d = grp_to(t)
            fill(d, send)
            grp_copy(send.at[d], recv.at[mq], gssem.at[phase], grsem.at[phase], d).start()
            return 0

        lax.fori_loop(1, groups, body, 0)

    def blocks_in(send, recv, phase):
        bytes_of(recv.at[0 : groups - 1], grsem.at[phase])
        bytes_of(send.at[0 : groups - 1], gssem.at[phase])
        return jnp.sum(recv[...].astype(F32), axis=0)

    def whole_out(value, send, recv, phase):
        send[...] = value.astype(BF16)
        recv[me] = value.astype(BF16)

        def body(t, _):
            d = row_to(t)
            row_copy(send, recv.at[me], gssem.at[phase], grsem.at[phase], d, core).start()
            return 0

        lax.fori_loop(1, ROWS, body, 0)

    def whole_in(recv, phase):
        bytes_of(recv.at[0 : ROWS - 1], grsem.at[phase])
        bytes_of(recv.at[0 : ROWS - 1], gssem.at[phase])
        return jnp.sum(recv[...].astype(F32), axis=0)

    def back_out(value, send, recv, phase):
        send[...] = value.astype(BF16)
        recv[mq] = value.astype(BF16)

        def body(t, _):
            d = grp_to(t)
            grp_copy(send, recv.at[mq], gssem.at[phase], grsem.at[phase], d).start()
            return 0

        lax.fori_loop(1, groups, body, 0)

    def back_in(recv, phase):
        bytes_of(recv.at[0 : groups - 1], grsem.at[phase])
        bytes_of(recv.at[0 : groups - 1], gssem.at[phase])

    proj = nt(nrm[1], gproj[1])
    for g in range(5):
        pay[g * 128 : g * 128 + 128, :] = proj[:, g * 128 : g * 128 + 128]
    pay[768:896, :] = nt(mdl[0], gup[0])
    pay[896:1024, :] = nt(nrm[0], gproj[0, 512:640, :])
    vectors((gacc[1], macc[1], macc[0]))
    blocks_out(a2s, a2r, 0, 64)

    gathered(recv1.at[3], 6)
    backward_channels(0, recv1.at[3], send2.at[3])
    give_back(send2.at[3], recv2.at[3], 7)
    left(1, send1.at[3], 6)
    whole_out(blocks_in(a2s, a2r, 0), b2s, b2r, 1)

    def fifth(i, chain, part):
        out[i] = lower(0, i, chain, part, w1).astype(F32).T.astype(BF16)

    for chain in range(2):
        returned(chain, recv2.at[3], 7, (s_a, s_b))
        tiles(chain, fifth)
    gave(send2.at[3], 7)
    stores = [pltpu.make_async_copy(out.at[mine], out_to.at[0, mine], osem.at[0])]
    stores[0].start()
    swap_back = swap(3, out.at[theirs], out_to.at[0, mine])
    swap_back.start()

    def store(n, a, b):
        stores.append(pltpu.make_async_copy(a, b, osem.at[n]))
        stores[-1].start()

    proj = nt(nrm[0], gproj[0, 0:512, :])
    for g in range(4):
        pay[g * 128 : g * 128 + 128, :] = proj[:, g * 128 : g * 128 + 128]
    vectors((gacc[0],))
    blocks_out(a1s, a1r, 3, 32)

    total = whole_in(b2r, 1)
    back_out(total[0:64], c2s, c2r, 2)
    o_n2[...] = total[64:65] * factor
    o_m2[...] = total[65:66] * factor
    o_m1[...] = total[66:67] * factor
    store(1, o_n2, n2_to)
    store(2, o_m2, m2_to)
    store(3, o_m1, m1_to)

    whole_out(blocks_in(a1s, a1r, 3), b1s, b1r, 4)
    back_in(c2r, 2)
    sums = c2r[...].reshape(1024, TILE).astype(F32) * factor
    for g in range(5):
        o_p2[:, g * 128 : g * 128 + 128] = sums[g * 128 : g * 128 + 128]
    o_f2[...] = sums[640:768]
    o_f1[...] = sums[768:896]
    o_p1[:, 512:640] = sums[896:1024]
    store(4, o_p2, p2_to)
    store(5, o_f2, f2_to)
    store(6, o_f1, f1_to)

    total = whole_in(b1r, 4)
    back_out(total[0:32], c1s, c1r, 5)
    o_n1[...] = total[32:33] * factor
    store(7, o_n1, n1_to)
    back_in(c1r, 5)
    sums = c1r[...].reshape(512, TILE).astype(F32) * factor
    for g in range(4):
        o_p1[:, g * 128 : g * 128 + 128] = sums[g * 128 : g * 128 + 128]

    store(8, o_p1, p1_to)
    for copy in stores:
        copy.wait()
    swap_back.wait()


def hand_on(*refs):
    froms, tos, held, sems = refs[:9], refs[9:18], refs[18:27], refs[27]
    loads = [pltpu.make_async_copy(a, b, sems.at[0, n]) for n, (a, b) in enumerate(zip(froms, held))]
    stores = [pltpu.make_async_copy(a, b, sems.at[1, n]) for n, (a, b) in enumerate(zip(held, tos))]
    for load in loads:
        load.start()
    for load, store in zip(loads, stores):
        load.wait()
        store.start()
    for store in stores:
        store.wait()


def on_device(groups, factor, pm, ct, mask, n1, w1, m1, f1, n2, w2, m2, f2):
    wide = (1, TILE)
    shapes = [
        (pm.shape, BF16),
        (wide, F32), ((TILE, 640), F32), (wide, F32), ((TILE, TILE), F32),
        (wide, F32), ((TILE, 640), F32), (wide, F32), ((TILE, TILE), F32),
    ]
    tile = (OWN, TILE, TILE)
    lane = (TILE, OWN * TILE)
    loaded = [
        (pm.shape[1:], BF16), (ct.shape[1:], BF16), ((2,) + mask.shape, jnp.int32),
        (wide, F32), ((TILE, 640), BF16), (wide, F32), ((TILE, TILE), BF16),
        (wide, F32), ((TILE, 640), BF16), (wide, F32), ((TILE, TILE), BF16),
    ]
    scratch = [pltpu.VMEM(s, d) for s, d in loaded + [(pm.shape[1:], BF16)] + shapes[1:]] + [
        pltpu.VMEM((2, 640, TILE), BF16),
        pltpu.VMEM((2, TILE, TILE), BF16),
        pltpu.VMEM((2, TILE, TILE), F32),
        pltpu.VMEM((2, TILE, TILE), F32),
        pltpu.VMEM((OWN, 1, TILE), F32),
        pltpu.VMEM(tile, F32),
        pltpu.VMEM((2,) + tile, F32),
        pltpu.VMEM((2, OWN, 1, TILE), F32),
        pltpu.VMEM((2,) + lane, BF16),
        pltpu.VMEM((2, 4) + tile, F32),
        pltpu.VMEM((2,) + tile, F32),
        pltpu.VMEM((2,) + tile, F32),
        pltpu.VMEM((2, OWN, 1, TILE), F32),
        pltpu.VMEM((2,) + lane, BF16),
        pltpu.VMEM((2,) + tile, F32),
        pltpu.VMEM((2,) + lane, BF16),
        pltpu.VMEM((2, 640, OWN * TILE), BF16),
        pltpu.VMEM((2,) + tile, F32),
        pltpu.VMEM((2, PART * TILE, TILE), F32),
        pltpu.VMEM((2, PART * TILE, TILE), F32),
        pltpu.VMEM((2,) + tile, BF16),
        pltpu.VMEM((2,) + tile, BF16),
        pltpu.VMEM((2, TILE, TILE), F32),
        pltpu.VMEM((2, TILE, TILE), F32),
        pltpu.VMEM((1024, TILE), F32),
        pltpu.VMEM((16, TILE), F32),
        pltpu.VMEM((4, 2 * ROWS, 64, TILE), BF16),
        pltpu.VMEM((4, 2 * ROWS, 64, TILE), BF16),
        pltpu.VMEM((4, 2 * ROWS, 32, TILE), BF16),
        pltpu.VMEM((4, 2 * ROWS, 32, TILE), BF16),
        pltpu.VMEM((16, 80, TILE), BF16),
        pltpu.VMEM((16, 80, TILE), BF16),
        pltpu.VMEM((80, TILE), BF16),
        pltpu.VMEM((ROWS, 80, TILE), BF16),
        pltpu.VMEM((64, TILE), BF16),
        pltpu.VMEM((16, 64, TILE), BF16),
        pltpu.VMEM((16, 48, TILE), BF16),
        pltpu.VMEM((16, 48, TILE), BF16),
        pltpu.VMEM((48, TILE), BF16),
        pltpu.VMEM((ROWS, 48, TILE), BF16),
        pltpu.VMEM((32, TILE), BF16),
        pltpu.VMEM((16, 32, TILE), BF16),
        pltpu.SemaphoreType.DMA((8, 2)),
        pltpu.SemaphoreType.DMA((8, 4)),
        pltpu.SemaphoreType.DMA((6,)),
        pltpu.SemaphoreType.DMA((6,)),
        pltpu.SemaphoreType.DMA((11,)),
        pltpu.SemaphoreType.DMA((9,)),
        pltpu.SemaphoreType.DMA((4,)),
        pltpu.SemaphoreType.DMA((4,)),
    ]
    anywhere = pl.BlockSpec(memory_space=pl.ANY)
    results = pl.pallas_call(
        functools.partial(kernel, groups, factor),
        out_shape=[jax.ShapeDtypeStruct(s, d) for s, d in shapes],
        in_specs=[anywhere] * 11,
        out_specs=[anywhere] * 9,
        scratch_shapes=scratch,
        compiler_params=pltpu.CompilerParams(
            collective_id=0, has_side_effects=True, vmem_limit_bytes=VMEM_BYTES
        ),
        name="triangle",
    )(
        pm, ct, mask,
        n1.reshape(wide), w1, m1.reshape(wide), f1,
        n2.reshape(wide), w2, m2.reshape(wide), f2,
    )
    results = pl.pallas_call(
        hand_on,
        out_shape=[jax.ShapeDtypeStruct(s, d) for s, d in shapes],
        in_specs=[anywhere] * 9,
        out_specs=[anywhere] * 9,
        scratch_shapes=[pltpu.VMEM(s, d) for s, d in shapes] + [pltpu.SemaphoreType.DMA((2, 9))],
        compiler_params=pltpu.CompilerParams(vmem_limit_bytes=VMEM_BYTES),
        name="hand_on",
    )(*results)
    flat = [r.reshape(TILE) if r.shape == wide else r for r in results]
    return tuple(flat)


def solution(mesh):
    groups = mesh.shape["rep"] * mesh.shape["cplx"]
    factor = 1.0 / math.sqrt(groups * TILE * TILE)
    blocks = P(("rep", "cplx"), "row", None, None)
    placed = (blocks, blocks, P(("rep", "cplx"), None)) + (P(),) * 8
    return jax.shard_map(
        functools.partial(on_device, groups, factor),
        mesh=mesh,
        in_specs=placed,
        out_specs=(blocks,) + (P(),) * 8,
        check_vma=False,
    )
```

```python
import functools
import math

import jax
import jax.numpy as jnp
from jax import lax
from jax.experimental import pallas as pl
from jax.experimental.pallas import tpu as pltpu
from jax.sharding import PartitionSpec as P

EPS = 1e-05
MESH = pl.DeviceIdType.MESH
F32 = jnp.float32
BF16 = jnp.bfloat16
ROWS = 16
TILE = 128
VMEM_BYTES = 63 * 1024 * 1024
OWN = 8
PART = 4


def nn(a, b):
    return lax.dot_general(a, b, (((1,), (0,)), ((), ())), preferred_element_type=F32)


def nt(a, b):
    return lax.dot_general(a, b, (((1,), (1,)), ((), ())), preferred_element_type=F32)


def turn(a):
    return a.astype(F32).T.astype(BF16)


def tn(a, b):
    return nn(turn(a), b)


def sigmoid(a):
    return 0.5 * jnp.tanh(0.5 * a) + 0.5


def mean0(a):
    return jnp.mean(a, axis=0, keepdims=True)


def normalize(a):
    centered = a - mean0(a)
    inv = lax.rsqrt(mean0(centered * centered) + EPS)
    return centered * inv, inv


def norm_back(e, standard, inv):
    return inv * (e - mean0(e) - standard * mean0(e * standard))


def kernel(
    groups, factor,
    pm_in, ct_in, mask_in, n1_in, w1_in, m1_in, f1_in, n2_in, w2_in, m2_in, f2_in,
    out_to, n1_to, p1_to, m1_to, f1_to, n2_to, p2_to, m2_to, f2_to, c1r,
    pm, ct, masks, n1, w1, m1, f1, n2, w2, m2, f2,
    out, o_n1, o_p1, o_m1, o_f1, o_n2, o_p2, o_m2, o_f2,
    wt, ft, ngain, mgain, rowm,
    xt, std, inv, nrm, cf, gate, ph, minv, mdl, upd, gup, gproj, inc,
    s_a, s_b, ch_l, ch_r,
    gacc, macc, pay, vec,
    send2, recv2, send1, recv1,
    a2s, a2r, b2n, b2f, c2s, c2r, a1s, a1r, b1s, b1r, c1s,
    ssem, rsem, gssem, grsem, isem, osem, xsem, ysem,
):
    me = lax.axis_index("row")
    my_x, my_z = me // 8, lax.rem(me, 8)
    my_rep, my_cplx = lax.axis_index("rep"), lax.axis_index("cplx")
    side, core = my_rep // 2, lax.rem(my_rep, 2)
    mate = 1 - core
    mq = my_rep * 4 + my_cplx

    def offsets(t):
        n = lax.rem(t - 1, 8)
        return 1 - (t - 1) // 8, lax.rem(12 + (2 * lax.rem(n, 2) - 1) * ((n + 1) // 2), 8)

    def row_to(t):
        dx, dz = offsets(t)
        return lax.rem(my_x + dx, 2) * 8 + lax.rem(my_z + dz, 8)

    def row_from(t):
        dx, dz = offsets(t)
        return lax.rem(my_x + dx, 2) * 8 + lax.rem(my_z + 8 - dz, 8)

    def grp_offsets(t):
        a, n = 3 - (t - 1) // 4, lax.rem(t - 1, 4)
        return a, lax.rem(6 + (2 * lax.rem(n, 2) - 1) * ((n + 1) // 2), 4)

    def grp_at(a, dy):
        r = lax.rem(side + a // 2, 2) * 2 + lax.rem(core + lax.rem(a, 2), 2)
        return r * 4 + lax.rem(my_cplx + dy, 4)

    def grp_to(t):
        a, dy = grp_offsets(t)
        return grp_at(a, dy)

    def grp_from(t):
        a, dy = grp_offsets(t)
        return grp_at(a, 4 - dy)

    def row_id(d, h):
        return {"rep": side * 2 + h, "row": d}

    def grp_id(d):
        return {"rep": d // 4, "cplx": lax.rem(d, 4)}

    barrier = pltpu.get_barrier_semaphore()

    def greet_row(t, _):
        for h in range(2):
            pl.semaphore_signal(barrier, inc=1, device_id=row_id(row_to(t), h), device_id_type=MESH)
        return 0

    def greet_grp(t, _):
        pl.semaphore_signal(barrier, inc=1, device_id=grp_id(grp_to(t)), device_id_type=MESH)
        return 0

    mine, theirs = pl.ds(core * PART, PART), pl.ds(mate * PART, PART)
    loads = [
        pltpu.make_async_copy(a, b, isem.at[n])
        for n, (a, b) in enumerate((
            (pm_in.at[0, mine], pm.at[mine]), (w1_in, w1), (n1_in, n1), (mask_in, masks.at[core]),
            (f1_in, f1), (m1_in, m1), (w2_in, w2), (n2_in, n2),
            (f2_in, f2), (m2_in, m2), (ct_in.at[0, mine], ct.at[mine]),
        ))
    ]
    for load in loads:
        load.start()
    lax.fori_loop(1, ROWS, greet_row, 0, unroll=15)
    lax.fori_loop(1, groups, greet_grp, 0, unroll=15)

    def swap(n, src, dst):
        return pltpu.make_async_remote_copy(
            src_ref=src, dst_ref=dst, send_sem=xsem.at[n], recv_sem=ysem.at[n],
            device_id=row_id(me, mate), device_id_type=MESH)

    def row_copy(src, dst, send_sem, recv_sem, d, h):
        return pltpu.make_async_remote_copy(
            src_ref=src, dst_ref=dst, send_sem=send_sem, recv_sem=recv_sem,
            device_id=row_id(d, h), device_id_type=MESH)

    def grp_copy(src, dst, send_sem, recv_sem, d):
        return pltpu.make_async_remote_copy(
            src_ref=src, dst_ref=dst, send_sem=send_sem, recv_sem=recv_sem,
            device_id=grp_id(d), device_id_type=MESH)

    def bytes_of(ref, sem):
        pltpu.make_async_copy(ref, ref, sem).wait()

    def lanes(i):
        return pl.ds(pl.multiple_of(i * TILE, TILE), TILE)

    def tiles(chain, body):
        def step(i, _):
            body(chain * PART + i, chain, i)
            return 0

        lax.fori_loop(0, PART, step, 0, unroll=4)

    def scatter(chain, stages, send, recv, phase):
        base = chain * ROWS
        mine_there = core * ROWS + me
        for n, stage in enumerate(stages):
            whole = stage[chain].reshape(ROWS, 32, TILE).astype(BF16)
            send[pl.ds(base, ROWS), n * 32 : n * 32 + 32, :] = whole

        def post(d):
            row_copy(send.at[base + d], recv.at[mine_there], ssem.at[phase, chain],
                     rsem.at[phase, 0], d, chain).start()

        def body(t, _):
            post(row_to(t))
            return 0

        lax.fori_loop(1, ROWS, body, 0, unroll=15)

        @pl.when(core == chain)
        def _():
            recv[mine_there] = send[base + me]

        @pl.when(core != chain)
        def _():
            post(me)

    def left(chain, send, phase):
        @pl.when(core == chain)
        def _():
            bytes_of(send.at[0 : ROWS - 1], ssem.at[phase, chain])

        @pl.when(core != chain)
        def _():
            bytes_of(send.at[0:ROWS], ssem.at[phase, chain])

    def give_back(send, recv, phase):
        mine_there = core * ROWS + me

        def post(d, h):
            column = core * 2 + lax.rem(d // 8 + my_x, 2)
            row_copy(send.at[h * ROWS + d], recv.at[mine_there], ssem.at[phase, 0],
                     rsem.at[phase, column], d, h).start()

        def body(t, _):
            d = row_to(t)
            post(d, 0)
            post(d, 1)
            return 0

        lax.fori_loop(1, ROWS, body, 0, unroll=15)
        post(me, mate)
        recv[mine_there] = send[mine_there]

    def gave(send, phase):
        bytes_of(send.at[0 : 2 * ROWS - 1], ssem.at[phase, 0])

    def gathered(recv, phase):
        bytes_of(recv.at[0 : 2 * ROWS - 1], rsem.at[phase, 0])

    def returned(chain, recv, phase, stages):
        def take(x):
            slots = pl.ds(chain * ROWS + x * 8, 8)
            rows = pl.ds(pl.multiple_of(x * 256, 256), 256)
            for n, stage in enumerate(stages):
                block = recv[slots, n * 32 : n * 32 + 32, :].astype(F32)
                stage[chain, rows, :] = block.reshape(256, TILE)

        bytes_of(recv.at[0:8], rsem.at[phase, chain * 2 + 1])
        take(1 - my_x)

        @pl.when(core == chain)
        def _():
            bytes_of(recv.at[0:7], rsem.at[phase, chain * 2])

        @pl.when(core != chain)
        def _():
            bytes_of(recv.at[0:8], rsem.at[phase, chain * 2])

        take(my_x)

    def strided(i):
        return pl.ds(i, TILE, stride=PART)

    low = lax.rem(lax.broadcasted_iota(jnp.int32, (TILE, TILE), 0), 8) < 4

    def halves(a, b):
        return (
            jnp.where(low, a, pltpu.roll(b, 4, 0)),
            jnp.where(low, pltpu.roll(a, TILE - 4, 0), b),
        )

    def four_of(recv, base, q):
        block = recv[:, pl.ds(pl.multiple_of(base + 16 * q, 16), 16), :].astype(F32)
        result = []
        for n in range(2):
            part = block[:, 8 * n : 8 * n + 8, :]
            a, b = part[0:ROWS].reshape(TILE, TILE), part[ROWS:].reshape(TILE, TILE)
            result += [m.astype(BF16) for m in halves(a, b)]
        return result

    def put_four(send, base, q, four):
        first, second = halves(four[0], four[1]), halves(four[2], four[3])
        where = pl.ds(pl.multiple_of(base + 16 * q, 16), 16)
        for h in range(2):
            both = [m[h].reshape(ROWS, 8, TILE) for m in (first, second)]
            send[h * ROWS : h * ROWS + ROWS, where, :] = jnp.concatenate(both, axis=1).astype(BF16)

    def fours(body):
        def step(q, _):
            body(q)
            return 0

        lax.fori_loop(0, 2, step, 0, unroll=2)

    def forward_channels(u, recv, send):
        def body(q):
            left, right = four_of(recv, 0, q), four_of(recv, 32, q)
            result = []
            for n in range(4):
                ch_l[u, 4 * q + n] = left[n]
                ch_r[u, 4 * q + n] = right[n]
                result.append(nt(left[n], right[n]) if u == 0 else tn(left[n], right[n]))
            put_four(send, 0, q, result)

        fours(body)

    def backward_channels(u, recv, send):
        def body(q):
            grads = four_of(recv, 0, q)
            lefts, rights = [], []
            for n in range(4):
                left, right, grad = ch_l[u, 4 * q + n], ch_r[u, 4 * q + n], grads[n]
                if u == 0:
                    lefts.append(nn(grad, right))
                    rights.append(tn(grad, left))
                else:
                    lefts.append(nt(right, grad))
                    rights.append(nn(left, grad))
            put_four(send, 0, q, lefts)
            put_four(send, 32, q, rights)

        fours(body)

    def front(u, i, chain, part, x):
        standard, inv_std = normalize(x)
        std[u, i] = standard
        inv[u, i] = inv_std
        normed = (standard * ngain[u]).astype(BF16)
        nrm[u, :, lanes(i)] = normed
        projected = nn(wt[u], normed)
        pair_mask = rowm[i] * masks[chain].astype(F32)
        s = sigmoid(projected[0:128])
        left = s * projected[128:256] * pair_mask
        cf[u, 0, i] = left * (1.0 - s)
        cf[u, 1, i] = s * pair_mask
        s_a[chain, strided(part), :] = left
        t = sigmoid(projected[256:384])
        right = t * projected[384:512] * pair_mask
        cf[u, 2, i] = right * (1.0 - t)
        cf[u, 3, i] = t * pair_mask
        s_b[chain, strided(part), :] = right
        gate[u, i] = sigmoid(projected[512:640])

    def finish(u, i, chain, part):
        prod_hat, mid_inv = normalize(s_a[chain, strided(part), :])
        middle = (prod_hat * mgain[u]).astype(BF16)
        update = nn(ft[u], middle)
        ph[u, i] = prod_hat
        minv[u, i] = mid_inv
        mdl[u, :, lanes(i)] = middle
        upd[u, i] = update
        return update, prod_hat, mid_inv

    def upper(u, i, chain, part, incoming, update, prod_hat, mid_inv, final):
        g = gate[u, i]
        inc[u, i] = incoming
        grad_update = (g * incoming).astype(BF16)
        gup[u, :, lanes(i)] = grad_update
        gproj[u, 512:640, lanes(i)] = (incoming * update * g * (1.0 - g)).astype(BF16)
        grad_middle = nn(final[...], grad_update)
        macc[u] += grad_middle * prod_hat
        s_b[chain, strided(part), :] = norm_back(grad_middle * mgain[u], prod_hat, mid_inv)

    def lower(u, i, chain, part, weight):
        grad_left, grad_right = s_a[chain, strided(part), :], s_b[chain, strided(part), :]
        gproj[u, 0:128, lanes(i)] = (grad_left * cf[u, 0, i]).astype(BF16)
        gproj[u, 128:256, lanes(i)] = (grad_left * cf[u, 1, i]).astype(BF16)
        gproj[u, 256:384, lanes(i)] = (grad_right * cf[u, 2, i]).astype(BF16)
        gproj[u, 384:512, lanes(i)] = (grad_right * cf[u, 3, i]).astype(BF16)
        grad_normed = nn(weight[...], gproj[u, :, lanes(i)])
        standard = std[u, i]
        gacc[u] += grad_normed * standard
        back = norm_back(grad_normed * ngain[u], standard, inv[u, i])
        return (inc[u, i] + back).astype(BF16)

    def spread(row):
        return jnp.broadcast_to(row[...], (TILE, TILE)).T

    def weights(u, w, n):
        for g in range(5):
            wt[u, g * 128 : g * 128 + 128, :] = turn(w[:, g * 128 : g * 128 + 128])
        ngain[u] = spread(n)

    for load in loads[0:4]:
        load.wait()
    weights(0, w1, n1)
    where = lax.broadcasted_iota(jnp.int32, (1, TILE), 1)

    def row_masks(chain):
        col_mask = masks[chain].astype(F32)
        for i in range(PART):
            here = where == me * OWN + core * PART + i
            picked = jnp.sum(jnp.where(here, col_mask, 0.0), axis=1, keepdims=True)
            rowm[chain * PART + i] = jnp.broadcast_to(picked, (1, TILE))

    row_masks(core)
    def first(i, chain, part):
        x = pm[i].astype(F32).T
        xt[i] = x
        front(0, i, chain, part, x)

    def scatter_first(chain):
        scatter(chain, (s_a, s_b), send2.at[0], recv2.at[0], 0)

    tiles(core, first)
    pl.semaphore_wait(barrier, 2 * (ROWS - 1) + groups - 1)
    swaps = [
        swap(0, pm_in.at[0, theirs], pm.at[mine]),
        swap(1, mask_in, masks.at[core]),
        swap(2, ct_in.at[0, theirs], ct.at[mine]),
    ]
    for copy in swaps:
        copy.start()

    @pl.when(core == 0)
    def _():
        scatter_first(0)

    swaps[0].wait()
    swaps[1].wait()
    row_masks(mate)
    tiles(mate, first)

    @pl.when(core == 1)
    def _():
        scatter_first(0)

    left(0, send2.at[0], 0)
    scatter_first(1)
    for load in loads[4:]:
        load.wait()
    swaps[2].wait()
    weights(1, w2, n2)
    for u, (f, m) in enumerate(((f1, m1), (f2, m2))):
        ft[u] = turn(f[...])
        mgain[u] = spread(m)
        gacc[u] = jnp.zeros((TILE, TILE), F32)
        macc[u] = jnp.zeros((TILE, TILE), F32)
    gathered(recv2.at[0], 0)
    forward_channels(0, recv2.at[0], send1.at[0])
    give_back(send1.at[0], recv1.at[0], 1)
    left(1, send2.at[0], 0)

    def second(i, chain, part):
        update, _, _ = finish(0, i, chain, part)
        first_out = (xt[i] + gate[0, i] * update).astype(BF16)
        front(1, i, chain, part, first_out.astype(F32))

    for chain in range(2):
        returned(chain, recv1.at[0], 1, (s_a,))
        tiles(chain, second)
        if chain == 1:
            left(0, send2.at[1], 2)
        scatter(chain, (s_a, s_b), send2.at[1], recv2.at[1], 2)
    gave(send1.at[0], 1)
    gathered(recv2.at[1], 2)
    forward_channels(1, recv2.at[1], send1.at[1])
    give_back(send1.at[1], recv1.at[1], 3)
    left(1, send2.at[1], 2)

    def third(i, chain, part):
        update, prod_hat, mid_inv = finish(1, i, chain, part)
        upper(1, i, chain, part, ct[i].astype(F32).T, update, prod_hat, mid_inv, f2)

    for chain in range(2):
        returned(chain, recv1.at[1], 3, (s_a,))
        tiles(chain, third)
        if chain == 1:
            left(0, send1.at[2], 4)
        scatter(chain, (s_b,), send1.at[2], recv1.at[2], 4)
    gave(send1.at[1], 3)
    pay[640:768, :] = nt(mdl[1], gup[1])
    gathered(recv1.at[2], 4)
    backward_channels(1, recv1.at[2], send2.at[2])
    give_back(send2.at[2], recv2.at[2], 5)
    left(1, send1.at[2], 4)

    def fourth(i, chain, part):
        first_grad = lower(1, i, chain, part, w2).astype(F32)
        upper(0, i, chain, part, first_grad, upd[0, i], ph[0, i], minv[0, i], f1)

    for chain in range(2):
        returned(chain, recv2.at[2], 5, (s_a, s_b))
        tiles(chain, fourth)
        if chain == 1:
            left(0, send1.at[3], 6)
        scatter(chain, (s_b,), send1.at[3], recv1.at[3], 6)
    gave(send2.at[2], 5)

    def vectors(values):
        vec[...] = jnp.zeros(vec.shape, F32)
        for n, value in enumerate(values):
            vec[n : n + 1, :] = jnp.sum(value.T, axis=0, keepdims=True)

    def blocks_out(send, recv, phase, block):
        def fill(d, ref):
            ref[d, 0:block, :] = pay[pl.ds(pl.multiple_of(d * block, block), block), :].astype(BF16)
            ref[d, block : block + 16, :] = vec[...].astype(BF16)

        fill(mq, recv)

        def body(t, _):
            d = grp_to(t)
            fill(d, send)
            grp_copy(send.at[d], recv.at[mq], gssem.at[phase], grsem.at[phase], d).start()
            return 0

        lax.fori_loop(1, groups, body, 0, unroll=15)

    def blocks_in(send, recv, phase):
        bytes_of(recv.at[0 : groups - 1], grsem.at[phase])
        bytes_of(send.at[0 : groups - 1], gssem.at[phase])
        return jnp.sum(recv[...].astype(F32), axis=0)

    def whole_out(value, send, recv, phase):
        send[...] = value.astype(BF16)
        recv[me] = value.astype(BF16)

        def body(t, _):
            d = row_to(t)
            row_copy(send, recv.at[me], gssem.at[phase], grsem.at[phase], d, core).start()
            return 0

        lax.fori_loop(1, ROWS, body, 0, unroll=15)

    def whole_in(recv, phase):
        bytes_of(recv.at[0 : ROWS - 1], grsem.at[phase])
        bytes_of(recv.at[0 : ROWS - 1], gssem.at[phase])
        return jnp.sum(recv[...].astype(F32), axis=0)

    def step_out(value, recv, step, phase):
        mine_there, peers = step_peers(step)
        recv[mine_there] = value.astype(BF16)
        for d in peers:
            row_copy(recv.at[mine_there], recv.at[mine_there], gssem.at[phase],
                     grsem.at[phase], d, core).start()

    def step_peers(step):
        near, far = my_x * 2 + lax.rem(my_z, 2), my_z // 2
        if step == 0:
            spots = [lax.rem(near + t, 4) for t in range(1, 4)]
            return near, [(p // 2) * 8 + far * 2 + lax.rem(p, 2) for p in spots]
        spots = [lax.rem(far + t, 4) for t in range(1, 4)]
        return far, [my_x * 8 + p * 2 + lax.rem(my_z, 2) for p in spots]

    def step_in(recv, phase):
        bytes_of(recv.at[0:3], grsem.at[phase])
        bytes_of(recv.at[0:3], gssem.at[phase])
        return jnp.sum(recv[...].astype(F32), axis=0)

    def back_out(value, send, recv, phase):
        send[...] = value.astype(BF16)
        recv[mq] = value.astype(BF16)

        def body(t, _):
            d = grp_to(t)
            grp_copy(send, recv.at[mq], gssem.at[phase], grsem.at[phase], d).start()
            return 0

        lax.fori_loop(1, groups, body, 0, unroll=15)

    def back_in(recv, phase):
        bytes_of(recv.at[0 : groups - 1], grsem.at[phase])
        bytes_of(recv.at[0 : groups - 1], gssem.at[phase])

    gathered(recv1.at[3], 6)
    backward_channels(0, recv1.at[3], send2.at[3])
    give_back(send2.at[3], recv2.at[3], 7)
    proj = nt(nrm[1], gproj[1])
    for g in range(5):
        pay[g * 128 : g * 128 + 128, :] = proj[:, g * 128 : g * 128 + 128]
    pay[768:896, :] = nt(mdl[0], gup[0])
    pay[896:1024, :] = nt(nrm[0], gproj[0, 512:640, :])
    vectors((gacc[1], macc[1], macc[0]))
    blocks_out(a2s, a2r, 0, 64)

    left(1, send1.at[3], 6)

    def fifth(i, chain, part):
        out[i] = lower(0, i, chain, part, w1).astype(F32).T.astype(BF16)

    for chain in range(2):
        returned(chain, recv2.at[3], 7, (s_a, s_b))
        tiles(chain, fifth)
        if chain == 0:
            step_out(blocks_in(a2s, a2r, 0), b2n, 0, 1)
    gave(send2.at[3], 7)
    stores = [pltpu.make_async_copy(out.at[mine], out_to.at[0, mine], osem.at[0])]
    stores[0].start()
    swap_back = swap(3, out.at[theirs], out_to.at[0, mine])
    swap_back.start()

    def store(n, a, b):
        stores.append(pltpu.make_async_copy(a, b, osem.at[n]))
        stores[-1].start()

    proj = nt(nrm[0], gproj[0, 0:512, :])
    for g in range(4):
        pay[g * 128 : g * 128 + 128, :] = proj[:, g * 128 : g * 128 + 128]
    vectors((gacc[0],))
    blocks_out(a1s, a1r, 3, 32)
    step_out(step_in(b2n, 1), b2f, 1, 6)

    whole_out(blocks_in(a1s, a1r, 3), b1s, b1r, 4)
    total = step_in(b2f, 6)
    back_out(total[0:64], c2s, c2r, 2)
    o_n2[...] = total[64:65] * factor
    o_m2[...] = total[65:66] * factor
    o_m1[...] = total[66:67] * factor
    store(1, o_n2, n2_to)
    store(2, o_m2, m2_to)
    store(3, o_m1, m1_to)
    total = whole_in(b1r, 4)
    c1s[...] = total[0:32].astype(BF16)
    own = pltpu.make_async_copy(c1s, c1r.at[mq], osem.at[9])
    own.start()

    def last(t, _):
        grp_copy(c1s, c1r.at[mq], gssem.at[5], grsem.at[5], grp_to(t)).start()
        return 0

    lax.fori_loop(1, groups, last, 0, unroll=15)
    o_n1[...] = total[32:33] * factor
    store(7, o_n1, n1_to)
    back_in(c2r, 2)
    sums = c2r[...].reshape(1024, TILE).astype(F32) * factor
    for g in range(5):
        o_p2[:, g * 128 : g * 128 + 128] = sums[g * 128 : g * 128 + 128]
    o_f2[...] = sums[640:768]
    o_f1[...] = sums[768:896]
    o_p1[...] = sums[896:1024]
    store(4, o_p2, p2_to)
    store(5, o_f2, f2_to)
    store(6, o_f1, f1_to)
    store(8, o_p1, p1_to)
    for copy in stores:
        copy.wait()
    own.wait()
    swap_back.wait()
    back_in(c1r, 5)


def hand_on(factor, *refs):
    froms, tos, held, sems = refs[:10], refs[10:19], refs[19:30], refs[30]
    whole = held[10]
    loads = [pltpu.make_async_copy(a, b, sems.at[0, n]) for n, (a, b) in enumerate(zip(froms, held))]
    last = 2
    stores = [
        pltpu.make_async_copy(whole if n == last else held[n], tos[n], sems.at[1, n])
        for n in range(9)
    ]
    for load in loads:
        load.start()
    for n in range(9):
        loads[n].wait()
        if n != last:
            stores[n].start()
    loads[9].wait()
    sums = held[9][...].reshape(512, TILE).astype(F32) * factor
    for g in range(4):
        whole[:, g * 128 : g * 128 + 128] = sums[g * 128 : g * 128 + 128]
    whole[:, 512:640] = held[last][...]
    stores[last].start()
    for store in stores:
        store.wait()


def on_device(groups, factor, pm, ct, mask, n1, w1, m1, f1, n2, w2, m2, f2):
    wide = (1, TILE)
    shapes = [
        (pm.shape, BF16),
        (wide, F32), ((TILE, 640), F32), (wide, F32), ((TILE, TILE), F32),
        (wide, F32), ((TILE, 640), F32), (wide, F32), ((TILE, TILE), F32),
    ]
    parts = list(shapes) + [((16, 32, TILE), BF16)]
    parts[2] = ((TILE, TILE), F32)
    tile = (OWN, TILE, TILE)
    lane = (TILE, OWN * TILE)
    loaded = [
        (pm.shape[1:], BF16), (ct.shape[1:], BF16), ((2,) + mask.shape, jnp.int32),
        (wide, F32), ((TILE, 640), BF16), (wide, F32), ((TILE, TILE), BF16),
        (wide, F32), ((TILE, 640), BF16), (wide, F32), ((TILE, TILE), BF16),
    ]
    scratch = [pltpu.VMEM(s, d) for s, d in loaded + [(pm.shape[1:], BF16)] + parts[1:9]] + [
        pltpu.VMEM((2, 640, TILE), BF16),
        pltpu.VMEM((2, TILE, TILE), BF16),
        pltpu.VMEM((2, TILE, TILE), F32),
        pltpu.VMEM((2, TILE, TILE), F32),
        pltpu.VMEM((OWN, 1, TILE), F32),
        pltpu.VMEM(tile, F32),
        pltpu.VMEM((2,) + tile, F32),
        pltpu.VMEM((2, OWN, 1, TILE), F32),
        pltpu.VMEM((2,) + lane, BF16),
        pltpu.VMEM((2, 4) + tile, F32),
        pltpu.VMEM((2,) + tile, F32),
        pltpu.VMEM((2,) + tile, F32),
        pltpu.VMEM((2, OWN, 1, TILE), F32),
        pltpu.VMEM((2,) + lane, BF16),
        pltpu.VMEM((2,) + tile, F32),
        pltpu.VMEM((2,) + lane, BF16),
        pltpu.VMEM((2, 640, OWN * TILE), BF16),
        pltpu.VMEM((2,) + tile, F32),
        pltpu.VMEM((2, PART * TILE, TILE), F32),
        pltpu.VMEM((2, PART * TILE, TILE), F32),
        pltpu.VMEM((2,) + tile, BF16),
        pltpu.VMEM((2,) + tile, BF16),
        pltpu.VMEM((2, TILE, TILE), F32),
        pltpu.VMEM((2, TILE, TILE), F32),
        pltpu.VMEM((1024, TILE), F32),
        pltpu.VMEM((16, TILE), F32),
        pltpu.VMEM((4, 2 * ROWS, 64, TILE), BF16),
        pltpu.VMEM((4, 2 * ROWS, 64, TILE), BF16),
        pltpu.VMEM((4, 2 * ROWS, 32, TILE), BF16),
        pltpu.VMEM((4, 2 * ROWS, 32, TILE), BF16),
        pltpu.VMEM((16, 80, TILE), BF16),
        pltpu.VMEM((16, 80, TILE), BF16),
        pltpu.VMEM((4, 80, TILE), BF16),
        pltpu.VMEM((4, 80, TILE), BF16),
        pltpu.VMEM((64, TILE), BF16),
        pltpu.VMEM((16, 64, TILE), BF16),
        pltpu.VMEM((16, 48, TILE), BF16),
        pltpu.VMEM((16, 48, TILE), BF16),
        pltpu.VMEM((48, TILE), BF16),
        pltpu.VMEM((ROWS, 48, TILE), BF16),
        pltpu.VMEM((32, TILE), BF16),
        pltpu.SemaphoreType.DMA((8, 2)),
        pltpu.SemaphoreType.DMA((8, 4)),
        pltpu.SemaphoreType.DMA((7,)),
        pltpu.SemaphoreType.DMA((7,)),
        pltpu.SemaphoreType.DMA((11,)),
        pltpu.SemaphoreType.DMA((10,)),
        pltpu.SemaphoreType.DMA((4,)),
        pltpu.SemaphoreType.DMA((4,)),
    ]
    anywhere = pl.BlockSpec(memory_space=pl.ANY)
    results = pl.pallas_call(
        functools.partial(kernel, groups, factor),
        out_shape=[jax.ShapeDtypeStruct(s, d) for s, d in parts],
        in_specs=[anywhere] * 11,
        out_specs=[anywhere] * 10,
        scratch_shapes=scratch,
        compiler_params=pltpu.CompilerParams(
            collective_id=0, has_side_effects=True, vmem_limit_bytes=VMEM_BYTES
        ),
        name="triangle",
    )(
        pm, ct, mask,
        n1.reshape(wide), w1, m1.reshape(wide), f1,
        n2.reshape(wide), w2, m2.reshape(wide), f2,
    )
    results = pl.pallas_call(
        functools.partial(hand_on, factor),
        out_shape=[jax.ShapeDtypeStruct(s, d) for s, d in shapes],
        in_specs=[anywhere] * 10,
        out_specs=[anywhere] * 9,
        scratch_shapes=[pltpu.VMEM(s, d) for s, d in parts + [shapes[2]]] + [pltpu.SemaphoreType.DMA((2, 10))],
        compiler_params=pltpu.CompilerParams(vmem_limit_bytes=VMEM_BYTES),
        name="hand_on",
    )(*results)
    flat = [r.reshape(TILE) if r.shape == wide else r for r in results]
    return tuple(flat)


def solution(mesh):
    groups = mesh.shape["rep"] * mesh.shape["cplx"]
    factor = 1.0 / math.sqrt(groups * TILE * TILE)
    blocks = P(("rep", "cplx"), "row", None, None)
    placed = (blocks, blocks, P(("rep", "cplx"), None)) + (P(),) * 8
    return jax.shard_map(
        functools.partial(on_device, groups, factor),
        mesh=mesh,
        in_specs=placed,
        out_specs=(blocks,) + (P(),) * 8,
        check_vma=False,
    )
```

```python
import functools
import math

import jax
import jax.numpy as jnp
from jax import lax
from jax.experimental import pallas as pl
from jax.experimental.pallas import tpu as pltpu
from jax.sharding import PartitionSpec as P

EPS = 1e-05
MESH = pl.DeviceIdType.MESH
F32 = jnp.float32
BF16 = jnp.bfloat16
ROWS = 16
TILE = 128
VMEM_BYTES = 63 * 1024 * 1024
OWN = 8
PART = 4


def nn(a, b):
    return lax.dot_general(a, b, (((1,), (0,)), ((), ())), preferred_element_type=F32)


def nt(a, b):
    return lax.dot_general(a, b, (((1,), (1,)), ((), ())), preferred_element_type=F32)


def turn(a):
    return a.astype(F32).T.astype(BF16)


def tn(a, b):
    return nn(turn(a), b)


def sigmoid(a):
    return 0.5 * jnp.tanh(0.5 * a) + 0.5


def mean0(a):
    return jnp.mean(a, axis=0, keepdims=True)


def normalize(a):
    centered = a - mean0(a)
    inv = lax.rsqrt(mean0(centered * centered) + EPS)
    return centered * inv, inv


def norm_back(e, standard, inv):
    return inv * (e - mean0(e) - standard * mean0(e * standard))


def kernel(
    groups, factor,
    pm_in, ct_in, mask_in, n1_in, w1_in, m1_in, f1_in, n2_in, w2_in, m2_in, f2_in,
    out_to, n1_to, p1_to, m1_to, f1_to, n2_to, p2_to, m2_to, f2_to, c1r,
    pm, ct, masks, n1, w1, m1, f1, n2, w2, m2, f2,
    out, o_n1, o_p1, o_m1, o_f1, o_n2, o_p2, o_m2, o_f2,
    wt, ft, ngain, mgain, rowm,
    xt, std, inv, nrm, cf, gate, ph, minv, mdl, upd, gup, gproj, inc,
    s_a, s_b, ch_l, ch_r,
    gacc, macc, pay, vec,
    send2, recv2, send1, recv1,
    a2s, a2r, b2n, b2f, c2s, c2r, a1s, a1r, b1s, b1r, c1s,
    ssem, rsem, gssem, grsem, isem, osem, xsem, ysem,
):
    me = lax.axis_index("row")
    my_x, my_z = me // 8, lax.rem(me, 8)
    my_rep, my_cplx = lax.axis_index("rep"), lax.axis_index("cplx")
    side, core = my_rep // 2, lax.rem(my_rep, 2)
    mate = 1 - core
    mq = my_rep * 4 + my_cplx

    def offsets(t):
        n = lax.rem(t - 1, 8)
        return 1 - (t - 1) // 8, lax.rem(12 + (2 * lax.rem(n, 2) - 1) * ((n + 1) // 2), 8)

    def row_to(t):
        dx, dz = offsets(t)
        return lax.rem(my_x + dx, 2) * 8 + lax.rem(my_z + dz, 8)

    def row_from(t):
        dx, dz = offsets(t)
        return lax.rem(my_x + dx, 2) * 8 + lax.rem(my_z + 8 - dz, 8)

    def grp_offsets(t):
        a, n = 3 - (t - 1) // 4, lax.rem(t - 1, 4)
        return a, lax.rem(6 + (2 * lax.rem(n, 2) - 1) * ((n + 1) // 2), 4)

    def grp_at(a, dy):
        r = lax.rem(side + a // 2, 2) * 2 + lax.rem(core + lax.rem(a, 2), 2)
        return r * 4 + lax.rem(my_cplx + dy, 4)

    def grp_to(t):
        a, dy = grp_offsets(t)
        return grp_at(a, dy)

    def grp_from(t):
        a, dy = grp_offsets(t)
        return grp_at(a, 4 - dy)

    def row_id(d, h):
        return {"rep": side * 2 + h, "row": d}

    def grp_id(d):
        return {"rep": d // 4, "cplx": lax.rem(d, 4)}

    barrier = pltpu.get_barrier_semaphore()

    def greet_row(t, _):
        for h in range(2):
            pl.semaphore_signal(barrier, inc=1, device_id=row_id(row_to(t), h), device_id_type=MESH)
        return 0

    def greet_grp(t, _):
        pl.semaphore_signal(barrier, inc=1, device_id=grp_id(grp_to(t)), device_id_type=MESH)
        return 0

    mine, theirs = pl.ds(core * PART, PART), pl.ds(mate * PART, PART)
    loads = [
        pltpu.make_async_copy(a, b, isem.at[n])
        for n, (a, b) in enumerate((
            (pm_in.at[0, mine], pm.at[mine]), (w1_in, w1), (n1_in, n1), (mask_in, masks.at[core]),
            (f1_in, f1), (m1_in, m1), (w2_in, w2), (n2_in, n2),
            (f2_in, f2), (m2_in, m2), (ct_in.at[0, mine], ct.at[mine]),
        ))
    ]
    for load in loads:
        load.start()
    lax.fori_loop(1, ROWS, greet_row, 0, unroll=15)
    lax.fori_loop(1, groups, greet_grp, 0, unroll=15)

    def swap(n, src, dst):
        return pltpu.make_async_remote_copy(
            src_ref=src, dst_ref=dst, send_sem=xsem.at[n], recv_sem=ysem.at[n],
            device_id=row_id(me, mate), device_id_type=MESH)

    def row_copy(src, dst, send_sem, recv_sem, d, h):
        return pltpu.make_async_remote_copy(
            src_ref=src, dst_ref=dst, send_sem=send_sem, recv_sem=recv_sem,
            device_id=row_id(d, h), device_id_type=MESH)

    def grp_copy(src, dst, send_sem, recv_sem, d):
        return pltpu.make_async_remote_copy(
            src_ref=src, dst_ref=dst, send_sem=send_sem, recv_sem=recv_sem,
            device_id=grp_id(d), device_id_type=MESH)

    def bytes_of(ref, sem):
        pltpu.make_async_copy(ref, ref, sem).wait()

    def lanes(i):
        return pl.ds(pl.multiple_of(i * TILE, TILE), TILE)

    def tiles(chain, body):
        def step(i, _):
            body(chain * PART + i, chain, i)
            return 0

        lax.fori_loop(0, PART, step, 0, unroll=4)

    def scatter(chain, stages, send, recv, phase):
        base = chain * ROWS
        mine_there = core * ROWS + me
        for n, stage in enumerate(stages):
            whole = stage[chain].reshape(ROWS, 32, TILE).astype(BF16)
            send[pl.ds(base, ROWS), n * 32 : n * 32 + 32, :] = whole

        def post(d, n):
            row_copy(send.at[base + d], recv.at[mine_there], ssem.at[phase, chain * 2 + n],
                     rsem.at[phase, 0], d, chain).start()

        def body_far(t, _):
            post(row_to(t), 0)
            return 0

        def body_near(t, _):
            post(row_to(t), 1)
            return 0

        lax.fori_loop(1, 9, body_far, 0, unroll=8)
        lax.fori_loop(9, ROWS, body_near, 0, unroll=7)

        @pl.when(core == chain)
        def _():
            recv[mine_there] = send[base + me]

        @pl.when(core != chain)
        def _():
            post(me, 1)

    def left_far(chain, send, phase):
        bytes_of(send.at[0:8], ssem.at[phase, chain * 2])

    def left_near(chain, send, phase):
        @pl.when(core == chain)
        def _():
            bytes_of(send.at[0:7], ssem.at[phase, chain * 2 + 1])

        @pl.when(core != chain)
        def _():
            bytes_of(send.at[0:8], ssem.at[phase, chain * 2 + 1])

    def left(send, phase):
        left_near(0, send, phase)
        left_far(1, send, phase)
        left_near(1, send, phase)

    def give_back(send, recv, phase):
        mine_there = core * ROWS + me

        def post(d, h):
            column = core * 2 + lax.rem(d // 8 + my_x, 2)
            row_copy(send.at[h * ROWS + d], recv.at[mine_there], ssem.at[phase, 0],
                     rsem.at[phase, column], d, h).start()

        def body(t, _):
            d = row_to(t)
            post(d, 0)
            post(d, 1)
            return 0

        lax.fori_loop(1, ROWS, body, 0, unroll=15)
        post(me, mate)
        recv[mine_there] = send[mine_there]

    def gave(send, phase):
        bytes_of(send.at[0 : 2 * ROWS - 1], ssem.at[phase, 0])

    def gathered(recv, phase):
        bytes_of(recv.at[0 : 2 * ROWS - 1], rsem.at[phase, 0])

    def returned(chain, recv, phase, stages):
        def take(x):
            slots = pl.ds(chain * ROWS + x * 8, 8)
            rows = pl.ds(pl.multiple_of(x * 256, 256), 256)
            for n, stage in enumerate(stages):
                block = recv[slots, n * 32 : n * 32 + 32, :].astype(F32)
                stage[chain, rows, :] = block.reshape(256, TILE)

        bytes_of(recv.at[0:8], rsem.at[phase, chain * 2 + 1])
        take(1 - my_x)

        @pl.when(core == chain)
        def _():
            bytes_of(recv.at[0:7], rsem.at[phase, chain * 2])

        @pl.when(core != chain)
        def _():
            bytes_of(recv.at[0:8], rsem.at[phase, chain * 2])

        take(my_x)

    def strided(i):
        return pl.ds(i, TILE, stride=PART)

    low = lax.rem(lax.broadcasted_iota(jnp.int32, (TILE, TILE), 0), 8) < 4

    def halves(a, b):
        return (
            jnp.where(low, a, pltpu.roll(b, 4, 0)),
            jnp.where(low, pltpu.roll(a, TILE - 4, 0), b),
        )

    def four_of(recv, base, q):
        block = recv[:, pl.ds(pl.multiple_of(base + 16 * q, 16), 16), :].astype(F32)
        result = []
        for n in range(2):
            part = block[:, 8 * n : 8 * n + 8, :]
            a, b = part[0:ROWS].reshape(TILE, TILE), part[ROWS:].reshape(TILE, TILE)
            result += [m.astype(BF16) for m in halves(a, b)]
        return result

    def put_four(send, base, q, four):
        first, second = halves(four[0], four[1]), halves(four[2], four[3])
        where = pl.ds(pl.multiple_of(base + 16 * q, 16), 16)
        for h in range(2):
            both = [m[h].reshape(ROWS, 8, TILE) for m in (first, second)]
            send[h * ROWS : h * ROWS + ROWS, where, :] = jnp.concatenate(both, axis=1).astype(BF16)

    def fours(body):
        def step(q, _):
            body(q)
            return 0

        lax.fori_loop(0, 2, step, 0, unroll=2)

    def forward_channels(u, recv, send):
        def body(q):
            left, right = four_of(recv, 0, q), four_of(recv, 32, q)
            result = []
            for n in range(4):
                ch_l[u, 4 * q + n] = left[n]
                ch_r[u, 4 * q + n] = right[n]
                result.append(nt(left[n], right[n]) if u == 0 else tn(left[n], right[n]))
            put_four(send, 0, q, result)

        fours(body)

    def backward_channels(u, recv, send):
        def body(q):
            grads = four_of(recv, 0, q)
            lefts, rights = [], []
            for n in range(4):
                left, right, grad = ch_l[u, 4 * q + n], ch_r[u, 4 * q + n], grads[n]
                if u == 0:
                    lefts.append(nn(grad, right))
                    rights.append(tn(grad, left))
                else:
                    lefts.append(nt(right, grad))
                    rights.append(nn(left, grad))
            put_four(send, 0, q, lefts)
            put_four(send, 32, q, rights)

        fours(body)

    def front(u, i, chain, part, x):
        standard, inv_std = normalize(x)
        std[u, i] = standard
        inv[u, i] = inv_std
        normed = (standard * ngain[u]).astype(BF16)
        nrm[u, :, lanes(i)] = normed
        projected = nn(wt[u], normed)
        pair_mask = rowm[i] * masks[chain].astype(F32)
        s = sigmoid(projected[0:128])
        left = s * projected[128:256] * pair_mask
        cf[u, 0, i] = left * (1.0 - s)
        cf[u, 1, i] = s * pair_mask
        s_a[chain, strided(part), :] = left
        t = sigmoid(projected[256:384])
        right = t * projected[384:512] * pair_mask
        cf[u, 2, i] = right * (1.0 - t)
        cf[u, 3, i] = t * pair_mask
        s_b[chain, strided(part), :] = right
        gate[u, i] = sigmoid(projected[512:640])

    def finish(u, i, chain, part):
        prod_hat, mid_inv = normalize(s_a[chain, strided(part), :])
        middle = (prod_hat * mgain[u]).astype(BF16)
        update = nn(ft[u], middle)
        ph[u, i] = prod_hat
        minv[u, i] = mid_inv
        mdl[u, :, lanes(i)] = middle
        upd[u, i] = update
        return update, prod_hat, mid_inv

    def upper(u, i, chain, part, incoming, update, prod_hat, mid_inv, final):
        g = gate[u, i]
        inc[u, i] = incoming
        grad_update = (g * incoming).astype(BF16)
        gup[u, :, lanes(i)] = grad_update
        gproj[u, 512:640, lanes(i)] = (incoming * update * g * (1.0 - g)).astype(BF16)
        grad_middle = nn(final[...], grad_update)
        macc[u] += grad_middle * prod_hat
        s_b[chain, strided(part), :] = norm_back(grad_middle * mgain[u], prod_hat, mid_inv)

    def lower(u, i, chain, part, weight):
        grad_left, grad_right = s_a[chain, strided(part), :], s_b[chain, strided(part), :]
        gproj[u, 0:128, lanes(i)] = (grad_left * cf[u, 0, i]).astype(BF16)
        gproj[u, 128:256, lanes(i)] = (grad_left * cf[u, 1, i]).astype(BF16)
        gproj[u, 256:384, lanes(i)] = (grad_right * cf[u, 2, i]).astype(BF16)
        gproj[u, 384:512, lanes(i)] = (grad_right * cf[u, 3, i]).astype(BF16)
        grad_normed = nn(weight[...], gproj[u, :, lanes(i)])
        standard = std[u, i]
        gacc[u] += grad_normed * standard
        back = norm_back(grad_normed * ngain[u], standard, inv[u, i])
        return (inc[u, i] + back).astype(BF16)

    def spread(row):
        return jnp.broadcast_to(row[...], (TILE, TILE)).T

    def weights(u, w, n):
        for g in range(5):
            wt[u, g * 128 : g * 128 + 128, :] = turn(w[:, g * 128 : g * 128 + 128])
        ngain[u] = spread(n)

    for load in loads[0:4]:
        load.wait()
    weights(0, w1, n1)
    where = lax.broadcasted_iota(jnp.int32, (1, TILE), 1)

    def row_masks(chain):
        col_mask = masks[chain].astype(F32)
        for i in range(PART):
            here = where == me * OWN + core * PART + i
            picked = jnp.sum(jnp.where(here, col_mask, 0.0), axis=1, keepdims=True)
            rowm[chain * PART + i] = jnp.broadcast_to(picked, (1, TILE))

    row_masks(core)
    def first(i, chain, part):
        x = pm[i].astype(F32).T
        xt[i] = x
        front(0, i, chain, part, x)

    def scatter_first(chain):
        scatter(chain, (s_a, s_b), send2.at[0], recv2.at[0], 0)

    tiles(core, first)
    pl.semaphore_wait(barrier, 2 * (ROWS - 1) + groups - 1)
    swaps = [
        swap(0, pm_in.at[0, theirs], pm.at[mine]),
        swap(1, mask_in, masks.at[core]),
        swap(2, ct_in.at[0, theirs], ct.at[mine]),
    ]
    for copy in swaps:
        copy.start()

    @pl.when(core == 0)
    def _():
        scatter_first(0)

    swaps[0].wait()
    swaps[1].wait()
    row_masks(mate)
    tiles(mate, first)

    @pl.when(core == 1)
    def _():
        scatter_first(0)

    left_far(0, send2.at[0], 0)
    scatter_first(1)
    for load in loads[4:]:
        load.wait()
    swaps[2].wait()
    weights(1, w2, n2)
    for u, (f, m) in enumerate(((f1, m1), (f2, m2))):
        ft[u] = turn(f[...])
        mgain[u] = spread(m)
        gacc[u] = jnp.zeros((TILE, TILE), F32)
        macc[u] = jnp.zeros((TILE, TILE), F32)
    gathered(recv2.at[0], 0)
    forward_channels(0, recv2.at[0], send1.at[0])
    give_back(send1.at[0], recv1.at[0], 1)
    left(send2.at[0], 0)

    def second(i, chain, part):
        update, _, _ = finish(0, i, chain, part)
        first_out = (xt[i] + gate[0, i] * update).astype(BF16)
        front(1, i, chain, part, first_out.astype(F32))

    for chain in range(2):
        returned(chain, recv1.at[0], 1, (s_a,))
        tiles(chain, second)
        if chain == 1:
            left_far(0, send2.at[1], 2)
        scatter(chain, (s_a, s_b), send2.at[1], recv2.at[1], 2)
    gave(send1.at[0], 1)
    gathered(recv2.at[1], 2)
    forward_channels(1, recv2.at[1], send1.at[1])
    give_back(send1.at[1], recv1.at[1], 3)
    left(send2.at[1], 2)

    def third(i, chain, part):
        update, prod_hat, mid_inv = finish(1, i, chain, part)
        upper(1, i, chain, part, ct[i].astype(F32).T, update, prod_hat, mid_inv, f2)

    for chain in range(2):
        returned(chain, recv1.at[1], 3, (s_a,))
        tiles(chain, third)
        if chain == 1:
            left_far(0, send1.at[2], 4)
        scatter(chain, (s_b,), send1.at[2], recv1.at[2], 4)
    gave(send1.at[1], 3)
    pay[640:768, :] = nt(mdl[1], gup[1])
    gathered(recv1.at[2], 4)
    backward_channels(1, recv1.at[2], send2.at[2])
    give_back(send2.at[2], recv2.at[2], 5)
    left(send1.at[2], 4)

    def fourth(i, chain, part):
        first_grad = lower(1, i, chain, part, w2).astype(F32)
        upper(0, i, chain, part, first_grad, upd[0, i], ph[0, i], minv[0, i], f1)

    for chain in range(2):
        returned(chain, recv2.at[2], 5, (s_a, s_b))
        tiles(chain, fourth)
        if chain == 1:
            left_far(0, send1.at[3], 6)
        scatter(chain, (s_b,), send1.at[3], recv1.at[3], 6)
    gave(send2.at[2], 5)

    def vectors(values):
        vec[...] = jnp.zeros(vec.shape, F32)
        for n, value in enumerate(values):
            vec[n : n + 1, :] = jnp.sum(value.T, axis=0, keepdims=True)

    def blocks_out(send, recv, phase, block):
        def fill(d, ref):
            ref[d, 0:block, :] = pay[pl.ds(pl.multiple_of(d * block, block), block), :].astype(BF16)
            ref[d, block : block + 16, :] = vec[...].astype(BF16)

        fill(mq, recv)

        def body(t, _):
            d = grp_to(t)
            fill(d, send)
            grp_copy(send.at[d], recv.at[mq], gssem.at[phase], grsem.at[phase], d).start()
            return 0

        lax.fori_loop(1, groups, body, 0, unroll=15)

    def blocks_in(send, recv, phase):
        bytes_of(recv.at[0 : groups - 1], grsem.at[phase])
        bytes_of(send.at[0 : groups - 1], gssem.at[phase])
        return jnp.sum(recv[...].astype(F32), axis=0)

    def whole_out(value, send, recv, phase):
        send[...] = value.astype(BF16)
        recv[me] = value.astype(BF16)

        def body(t, _):
            d = row_to(t)
            row_copy(send, recv.at[me], gssem.at[phase], grsem.at[phase], d, core).start()
            return 0

        lax.fori_loop(1, ROWS, body, 0, unroll=15)

    def whole_in(recv, phase):
        bytes_of(recv.at[0 : ROWS - 1], grsem.at[phase])
        bytes_of(recv.at[0 : ROWS - 1], gssem.at[phase])
        return jnp.sum(recv[...].astype(F32), axis=0)

    def step_out(value, recv, step, phase):
        mine_there, peers = step_peers(step)
        recv[mine_there] = value.astype(BF16)
        for d in peers:
            row_copy(recv.at[mine_there], recv.at[mine_there], gssem.at[phase],
                     grsem.at[phase], d, core).start()

    def step_peers(step):
        near, far = my_x * 2 + lax.rem(my_z, 2), my_z // 2
        if step == 0:
            spots = [lax.rem(near + t, 4) for t in range(1, 4)]
            return near, [(p // 2) * 8 + far * 2 + lax.rem(p, 2) for p in spots]
        spots = [lax.rem(far + t, 4) for t in range(1, 4)]
        return far, [my_x * 8 + p * 2 + lax.rem(my_z, 2) for p in spots]

    def step_in(recv, phase):
        bytes_of(recv.at[0:3], grsem.at[phase])
        bytes_of(recv.at[0:3], gssem.at[phase])
        return jnp.sum(recv[...].astype(F32), axis=0)

    def back_out(value, send, recv, phase):
        send[...] = value.astype(BF16)
        recv[mq] = value.astype(BF16)

        def body(t, _):
            d = grp_to(t)
            grp_copy(send, recv.at[mq], gssem.at[phase], grsem.at[phase], d).start()
            return 0

        lax.fori_loop(1, groups, body, 0, unroll=15)

    def back_in(recv, phase):
        bytes_of(recv.at[0 : groups - 1], grsem.at[phase])
        bytes_of(recv.at[0 : groups - 1], gssem.at[phase])

    gathered(recv1.at[3], 6)
    backward_channels(0, recv1.at[3], send2.at[3])
    give_back(send2.at[3], recv2.at[3], 7)
    proj = nt(nrm[1], gproj[1])
    for g in range(5):
        pay[g * 128 : g * 128 + 128, :] = proj[:, g * 128 : g * 128 + 128]
    pay[768:896, :] = nt(mdl[0], gup[0])
    pay[896:1024, :] = nt(nrm[0], gproj[0, 512:640, :])
    vectors((gacc[1], macc[1], macc[0]))
    blocks_out(a2s, a2r, 0, 64)

    left(send1.at[3], 6)

    def fifth(i, chain, part):
        out[i] = lower(0, i, chain, part, w1).astype(F32).T.astype(BF16)

    for chain in range(2):
        returned(chain, recv2.at[3], 7, (s_a, s_b))
        tiles(chain, fifth)
        half = slice(chain * 512, chain * 512 + 512)
        proj = nt(nrm[0, :, half], gproj[0, 0:512, half])
        for g in range(4):
            rows = slice(g * 128, g * 128 + 128)
            pay[rows, :] = proj[:, rows] if chain == 0 else pay[rows, :] + proj[:, rows]
        if chain == 0:
            step_out(blocks_in(a2s, a2r, 0), b2n, 0, 1)
    def store(n, a, b):
        stores.append(pltpu.make_async_copy(a, b, osem.at[n]))
        stores[-1].start()

    vectors((gacc[0],))
    blocks_out(a1s, a1r, 3, 32)
    gave(send2.at[3], 7)
    stores = [pltpu.make_async_copy(out.at[mine], out_to.at[0, mine], osem.at[0])]
    stores[0].start()
    swap_back = swap(3, out.at[theirs], out_to.at[0, mine])
    swap_back.start()
    step_out(step_in(b2n, 1), b2f, 1, 6)

    whole_out(blocks_in(a1s, a1r, 3), b1s, b1r, 4)
    total = step_in(b2f, 6)
    back_out(total[0:64], c2s, c2r, 2)
    o_n2[...] = total[64:65] * factor
    o_m2[...] = total[65:66] * factor
    o_m1[...] = total[66:67] * factor
    store(1, o_n2, n2_to)
    store(2, o_m2, m2_to)
    store(3, o_m1, m1_to)
    total = whole_in(b1r, 4)
    c1s[...] = total[0:32].astype(BF16)
    own = pltpu.make_async_copy(c1s, c1r.at[mq], osem.at[9])
    own.start()

    def last(t, _):
        grp_copy(c1s, c1r.at[mq], gssem.at[5], grsem.at[5], grp_to(t)).start()
        return 0

    lax.fori_loop(1, groups, last, 0, unroll=15)
    o_n1[...] = total[32:33] * factor
    store(7, o_n1, n1_to)
    back_in(c2r, 2)
    sums = c2r[...].reshape(1024, TILE).astype(F32) * factor
    for g in range(5):
        o_p2[:, g * 128 : g * 128 + 128] = sums[g * 128 : g * 128 + 128]
    o_f2[...] = sums[640:768]
    o_f1[...] = sums[768:896]
    o_p1[...] = sums[896:1024]
    store(4, o_p2, p2_to)
    store(5, o_f2, f2_to)
    store(6, o_f1, f1_to)
    store(8, o_p1, p1_to)
    for copy in stores:
        copy.wait()
    own.wait()
    swap_back.wait()
    back_in(c1r, 5)


def hand_on(factor, *refs):
    froms, tos, held, sems = refs[:10], refs[10:19], refs[19:30], refs[30]
    whole = held[10]
    loads = [pltpu.make_async_copy(a, b, sems.at[0, n]) for n, (a, b) in enumerate(zip(froms, held))]
    last = 2
    stores = [
        pltpu.make_async_copy(whole if n == last else held[n], tos[n], sems.at[1, n])
        for n in range(9)
    ]
    for load in loads:
        load.start()
    for n in range(9):
        loads[n].wait()
        if n != last:
            stores[n].start()
    loads[9].wait()
    sums = held[9][...].reshape(512, TILE).astype(F32) * factor
    for g in range(4):
        whole[:, g * 128 : g * 128 + 128] = sums[g * 128 : g * 128 + 128]
    whole[:, 512:640] = held[last][...]
    stores[last].start()
    for store in stores:
        store.wait()


def on_device(groups, factor, pm, ct, mask, n1, w1, m1, f1, n2, w2, m2, f2):
    wide = (1, TILE)
    shapes = [
        (pm.shape, BF16),
        (wide, F32), ((TILE, 640), F32), (wide, F32), ((TILE, TILE), F32),
        (wide, F32), ((TILE, 640), F32), (wide, F32), ((TILE, TILE), F32),
    ]
    parts = list(shapes) + [((16, 32, TILE), BF16)]
    parts[2] = ((TILE, TILE), F32)
    tile = (OWN, TILE, TILE)
    lane = (TILE, OWN * TILE)
    loaded = [
        (pm.shape[1:], BF16), (ct.shape[1:], BF16), ((2,) + mask.shape, jnp.int32),
        (wide, F32), ((TILE, 640), BF16), (wide, F32), ((TILE, TILE), BF16),
        (wide, F32), ((TILE, 640), BF16), (wide, F32), ((TILE, TILE), BF16),
    ]
    scratch = [pltpu.VMEM(s, d) for s, d in loaded + [(pm.shape[1:], BF16)] + parts[1:9]] + [
        pltpu.VMEM((2, 640, TILE), BF16),
        pltpu.VMEM((2, TILE, TILE), BF16),
        pltpu.VMEM((2, TILE, TILE), F32),
        pltpu.VMEM((2, TILE, TILE), F32),
        pltpu.VMEM((OWN, 1, TILE), F32),
        pltpu.VMEM(tile, F32),
        pltpu.VMEM((2,) + tile, F32),
        pltpu.VMEM((2, OWN, 1, TILE), F32),
        pltpu.VMEM((2,) + lane, BF16),
        pltpu.VMEM((2, 4) + tile, F32),
        pltpu.VMEM((2,) + tile, F32),
        pltpu.VMEM((2,) + tile, F32),
        pltpu.VMEM((2, OWN, 1, TILE), F32),
        pltpu.VMEM((2,) + lane, BF16),
        pltpu.VMEM((2,) + tile, F32),
        pltpu.VMEM((2,) + lane, BF16),
        pltpu.VMEM((2, 640, OWN * TILE), BF16),
        pltpu.VMEM((2,) + tile, F32),
        pltpu.VMEM((2, PART * TILE, TILE), F32),
        pltpu.VMEM((2, PART * TILE, TILE), F32),
        pltpu.VMEM((2,) + tile, BF16),
        pltpu.VMEM((2,) + tile, BF16),
        pltpu.VMEM((2, TILE, TILE), F32),
        pltpu.VMEM((2, TILE, TILE), F32),
        pltpu.VMEM((1024, TILE), F32),
        pltpu.VMEM((16, TILE), F32),
        pltpu.VMEM((4, 2 * ROWS, 64, TILE), BF16),
        pltpu.VMEM((4, 2 * ROWS, 64, TILE), BF16),
        pltpu.VMEM((4, 2 * ROWS, 32, TILE), BF16),
        pltpu.VMEM((4, 2 * ROWS, 32, TILE), BF16),
        pltpu.VMEM((16, 80, TILE), BF16),
        pltpu.VMEM((16, 80, TILE), BF16),
        pltpu.VMEM((4, 80, TILE), BF16),
        pltpu.VMEM((4, 80, TILE), BF16),
        pltpu.VMEM((64, TILE), BF16),
        pltpu.VMEM((16, 64, TILE), BF16),
        pltpu.VMEM((16, 48, TILE), BF16),
        pltpu.VMEM((16, 48, TILE), BF16),
        pltpu.VMEM((48, TILE), BF16),
        pltpu.VMEM((ROWS, 48, TILE), BF16),
        pltpu.VMEM((32, TILE), BF16),
        pltpu.SemaphoreType.DMA((8, 4)),
        pltpu.SemaphoreType.DMA((8, 4)),
        pltpu.SemaphoreType.DMA((7,)),
        pltpu.SemaphoreType.DMA((7,)),
        pltpu.SemaphoreType.DMA((11,)),
        pltpu.SemaphoreType.DMA((10,)),
        pltpu.SemaphoreType.DMA((4,)),
        pltpu.SemaphoreType.DMA((4,)),
    ]
    anywhere = pl.BlockSpec(memory_space=pl.ANY)
    results = pl.pallas_call(
        functools.partial(kernel, groups, factor),
        out_shape=[jax.ShapeDtypeStruct(s, d) for s, d in parts],
        in_specs=[anywhere] * 11,
        out_specs=[anywhere] * 10,
        scratch_shapes=scratch,
        compiler_params=pltpu.CompilerParams(
            collective_id=0, has_side_effects=True, vmem_limit_bytes=VMEM_BYTES
        ),
        name="triangle",
    )(
        pm, ct, mask,
        n1.reshape(wide), w1, m1.reshape(wide), f1,
        n2.reshape(wide), w2, m2.reshape(wide), f2,
    )
    results = pl.pallas_call(
        functools.partial(hand_on, factor),
        out_shape=[jax.ShapeDtypeStruct(s, d) for s, d in shapes],
        in_specs=[anywhere] * 10,
        out_specs=[anywhere] * 9,
        scratch_shapes=[pltpu.VMEM(s, d) for s, d in parts + [shapes[2]]] + [pltpu.SemaphoreType.DMA((2, 10))],
        compiler_params=pltpu.CompilerParams(vmem_limit_bytes=VMEM_BYTES),
        name="hand_on",
    )(*results)
    flat = [r.reshape(TILE) if r.shape == wide else r for r in results]
    return tuple(flat)


def solution(mesh):
    groups = mesh.shape["rep"] * mesh.shape["cplx"]
    factor = 1.0 / math.sqrt(groups * TILE * TILE)
    blocks = P(("rep", "cplx"), "row", None, None)
    placed = (blocks, blocks, P(("rep", "cplx"), None)) + (P(),) * 8
    return jax.shard_map(
        functools.partial(on_device, groups, factor),
        mesh=mesh,
        in_specs=placed,
        out_specs=(blocks,) + (P(),) * 8,
        check_vma=False,
    )
```
